32 devices in a mesh: dp: 4 (over z), tp: 4 (over x, core), expert: 2 (over y).
Axes of the slice: x: 2, y: 2, z: 4, core: 2. Of those that a mesh axis runs over, the one named last changes fastest.
Arguments:
- prefix_in: bfloat16 [8, 576, 2048], P('dp', 'expert'), may hold values from -6 to 6
- suffix_in: bfloat16 [8, 51, 1024], P(('dp', 'expert')), may hold values from -6 to 6
- noisy_actions: bfloat16 [8, 50, 32], P(('dp', 'expert')), may hold values from -6 to 6
- prefix_len: int32 [8], P('dp'), may hold values from 144 to 576, as said below
- action_live: int32 [8, 32], P(('dp', 'expert')), may hold values from 0 to 1, as said below
- pre_query: bfloat16 [2048, 2048], P(('dp', 'expert'), 'tp'), may hold values from -0.125 to 0.125
- pre_keyval: bfloat16 [2048, 512], P(('dp', 'expert')), may hold values from -0.125 to 0.125
- pre_output: bfloat16 [2048, 2048], P('tp', ('dp', 'expert')), may hold values from -1.5 to 1.5
- pre_gate: bfloat16 [2048, 16384], P(('dp', 'expert'), 'tp'), may hold values from -0.125 to 0.125
- pre_up: bfloat16 [2048, 16384], P(('dp', 'expert'), 'tp'), may hold values from -0.125 to 0.125
- pre_down: bfloat16 [16384, 2048], P('tp', ('dp', 'expert')), may hold values from -0.046875 to 0.046875
- pre_norm_attn: bfloat16 [2048], P(('dp', 'expert')), may hold values from 0.099609375 to 1.8984375
- pre_norm_ffn: bfloat16 [2048], P(('dp', 'expert')), may hold values from 0.099609375 to 1.8984375
- act_query: bfloat16 [1024, 2048], P(('dp', 'expert'), 'tp'), may hold values from -0.1875 to 0.1875
- act_keyval: bfloat16 [1024, 512], P(('dp', 'expert')), may hold values from -0.1875 to 0.1875
- act_output: bfloat16 [2048, 1024], P('tp', ('dp', 'expert')), may hold values from -1.5 to 1.5
- act_gate: bfloat16 [1024, 4096], P(('dp', 'expert'), 'tp'), may hold values from -0.1875 to 0.1875
- act_up: bfloat16 [1024, 4096], P(('dp', 'expert'), 'tp'), may hold values from -0.1875 to 0.1875
- act_down: bfloat16 [4096, 1024], P('tp', ('dp', 'expert')), may hold values from -0.09375 to 0.09375
- act_norm_attn: bfloat16 [1024], P(('dp', 'expert')), may hold values from 0.099609375 to 1.8984375
- act_norm_ffn: bfloat16 [1024], P(('dp', 'expert')), may hold values from 0.099609375 to 1.8984375
- action_embed: bfloat16 [32, 1024], P(('dp', 'expert')), may hold values from -1.5 to 1.5
- prefix_cot: bfloat16 [8, 576, 2048], P('dp', 'expert'), may hold values from -6 to 6
- suffix_cot: bfloat16 [8, 51, 1024], P(('dp', 'expert')), may hold values from -6 to 6
Outputs:
- prefix_out: bfloat16 [8, 576, 2048], P('dp', 'expert')
- suffix_out: bfloat16 [8, 51, 1024], P(('dp', 'expert'))
- prefix_in_grad: float32 [8, 576, 2048], P('dp', 'expert')
- suffix_in_grad: float32 [8, 51, 1024], P(('dp', 'expert'))
- pre_query_grad: float32 [2048, 2048], P(('dp', 'expert'), 'tp')
- pre_keyval_grad: float32 [2048, 512], P(('dp', 'expert'))
- pre_output_grad: float32 [2048, 2048], P('tp', ('dp', 'expert'))
- pre_gate_grad: float32 [2048, 16384], P(('dp', 'expert'), 'tp')
- pre_up_grad: float32 [2048, 16384], P(('dp', 'expert'), 'tp')
- pre_down_grad: float32 [16384, 2048], P('tp', ('dp', 'expert'))
- pre_norm_attn_grad: float32 [2048], P(('dp', 'expert'))
- pre_norm_ffn_grad: float32 [2048], P(('dp', 'expert'))
- act_query_grad: float32 [1024, 2048], P(('dp', 'expert'), 'tp')
- act_keyval_grad: float32 [1024, 512], P(('dp', 'expert'))
- act_output_grad: float32 [2048, 1024], P('tp', ('dp', 'expert'))
- act_gate_grad: float32 [1024, 4096], P(('dp', 'expert'), 'tp')
- act_up_grad: float32 [1024, 4096], P(('dp', 'expert'), 'tp')
- act_down_grad: float32 [4096, 1024], P('tp', ('dp', 'expert'))
- act_norm_attn_grad: float32 [1024], P(('dp', 'expert'))
- act_norm_ffn_grad: float32 [1024], P(('dp', 'expert'))
- action_embed_grad: float32 [32, 1024], P(('dp', 'expert'))
The draws below stay inside these ranges and needn't reach their ends.
Inputs may be any that keep to these rules, and one draw needn't show every extreme that they name: `prefix_len`: prefix positions at or beyond an item's length are never attended; among the items of each index of dp one has the full 576 and another 576 // 4. `action_live`: 1 marks a live action dimension; each item has 7 to 18 live ones, some item 7 and another 18.
All inputs are finite; a program needn't handle non-finite values.
Results may differ from the reference program's by a relative error of at most 0.014.
Values may be sent and summed in bfloat16 or wider, within the bound.
No kernel may reach another device: no remote copies, remote signals or barrier semaphores. Data moves between devices by JAX's collectives and lax.ppermute only.
A program may use at most 320 MiB of HBM per device.

```python
import jax
import jax.numpy as jnp
from jax import lax

D = 2048
FF = 16384
DA = 1024
FFA = 4096
HEADS = 8
HD = 256
ADIM = 32
HORIZON = 50
PREFIX = 576
SUFFIX = 51
ITEMS = 8
N_DP = 4


def draw_prefix_len(key, part):
    key = jax.random.fold_in(key, 11)
    first, second = jax.random.split(key)
    group = ITEMS // N_DP
    base = jax.random.randint(first, (ITEMS,), PREFIX // 4, PREFIX + 1)
    picked = jax.random.randint(second, (N_DP,), 0, group)
    chosen = jnp.repeat(picked, group)
    within = jnp.arange(ITEMS) % group
    lengths = jnp.where(within == chosen, PREFIX, base)
    lengths = jnp.where(within == (chosen + 1) % group, PREFIX // 4, lengths)
    return lengths.astype(jnp.int32)


def draw_action_live(key, part):
    key = jax.random.fold_in(key, 23)
    first, second, third = jax.random.split(key, 3)
    counts = jax.random.randint(first, (ITEMS,), 7, 19)
    fewest = jax.random.randint(second, (), 0, ITEMS)
    item_index = jnp.arange(ITEMS)
    counts = jnp.where(item_index == fewest, 7, counts)
    counts = jnp.where(item_index == (fewest + 1) % ITEMS, 18, counts)
    scores = jax.random.randint(third, (ITEMS, ADIM), 0, 1 << 20) * ADIM + jnp.arange(ADIM)[None, :]
    order = jnp.argsort(scores, axis=1, stable=True)
    ranks = jnp.argsort(order, axis=1, stable=True)
    return (ranks < counts[:, None]).astype(jnp.int32)


def level_of(rng, extent, shards, least, high):
    def one(dim, parts):
        steps = jax.random.uniform(jax.random.fold_in(jax.random.fold_in(rng, 6), dim), (parts,), jnp.float32, least / len(shards), high / len(shards))
        return jnp.repeat(jnp.exp(steps), extent[dim] // parts).reshape((-1,) + (1,) * (len(extent) - dim - 1))

    level = one(*shards[0])
    for cut in shards[1:]:
        level = level * one(*cut)
    return level


def noise(rng, shape, width, limit, cuts=(), held_as=jnp.bfloat16):
    drawn = jax.random.normal(rng, shape, jnp.float32) * width
    if len(cuts) > 0:
        drawn = level_of(rng, shape, cuts, -0.22, 0.18) * drawn
    return jnp.clip(drawn, min=-limit, max=limit).astype(held_as)


def setup_inputs(seed: int = 0) -> dict:
    key_list = jax.random.split(jax.random.key(seed), 25)
    prefix_in = noise(key_list[0], (ITEMS, PREFIX, D), 1.0, 6.0, ((0, 4), (1, 2)))
    suffix_in = noise(key_list[1], (ITEMS, SUFFIX, DA), 1.0, 6.0, ((0, 8),))
    noisy_actions = noise(key_list[2], (ITEMS, HORIZON, ADIM), 1.0, 6.0, ((0, 8),))
    prefix_len = draw_prefix_len(jax.random.fold_in(key_list[24], 71), 0)
    action_live = draw_action_live(jax.random.fold_in(key_list[24], 71), 0)
    pre_query = noise(key_list[5], (D, HEADS * HD), D ** -0.5, 0.125, ((0, 8), (1, 4)))
    pre_keyval = noise(key_list[6], (D, 2 * HD), D ** -0.5, 0.125, ((0, 8),))
    pre_output = noise(key_list[7], (HEADS * HD, D), (max(HEADS * HD * 4 // PREFIX, 1)) ** -0.5, 1.5, ((0, 4), (1, 8)))
    pre_gate = noise(key_list[8], (D, FF), D ** -0.5, 0.125, ((0, 8), (1, 4)))
    pre_up = noise(key_list[9], (D, FF), D ** -0.5, 0.125, ((0, 8), (1, 4)))
    pre_down = noise(key_list[10], (FF, D), FF ** -0.5, 0.046875, ((0, 4), (1, 8)))
    pre_norm_attn = jnp.clip(1.0 + 0.18 * jax.random.normal(key_list[11], (D,), jnp.float32), 0.099609375, 1.8984375).astype(jnp.bfloat16)
    pre_norm_ffn = jnp.clip(1.0 + 0.18 * jax.random.normal(key_list[12], (D,), jnp.float32), 0.099609375, 1.8984375).astype(jnp.bfloat16)
    act_query = noise(key_list[13], (DA, HEADS * HD), DA ** -0.5, 0.1875, ((0, 8), (1, 4)))
    act_keyval = noise(key_list[14], (DA, 2 * HD), DA ** -0.5, 0.1875, ((0, 8),))
    act_output = noise(key_list[15], (HEADS * HD, DA), (max(HEADS * HD * 4 // PREFIX, 1)) ** -0.5, 1.5, ((0, 4), (1, 8)))
    act_gate = noise(key_list[16], (DA, FFA), DA ** -0.5, 0.1875, ((0, 8), (1, 4)))
    act_up = noise(key_list[17], (DA, FFA), DA ** -0.5, 0.1875, ((0, 8), (1, 4)))
    act_down = noise(key_list[18], (FFA, DA), FFA ** -0.5, 0.09375, ((0, 4), (1, 8)))
    act_norm_attn = jnp.clip(1.0 + 0.18 * jax.random.normal(key_list[19], (DA,), jnp.float32), 0.099609375, 1.8984375).astype(jnp.bfloat16)
    act_norm_ffn = jnp.clip(1.0 + 0.18 * jax.random.normal(key_list[20], (DA,), jnp.float32), 0.099609375, 1.8984375).astype(jnp.bfloat16)
    action_embed = noise(key_list[21], (ADIM, DA), (ADIM // 2) ** -0.5, 1.5, ((0, 8),))
    prefix_cot = noise(key_list[22], (ITEMS, PREFIX, D), 1.0, 6.0, ((0, 4), (1, 2)))
    suffix_cot = noise(key_list[23], (ITEMS, SUFFIX, DA), 1.0, 6.0, ((0, 8),))
    return dict(prefix_in=prefix_in, suffix_in=suffix_in, noisy_actions=noisy_actions, prefix_len=prefix_len, action_live=action_live, pre_query=pre_query, pre_keyval=pre_keyval, pre_output=pre_output, pre_gate=pre_gate, pre_up=pre_up, pre_down=pre_down, pre_norm_attn=pre_norm_attn, pre_norm_ffn=pre_norm_ffn, act_query=act_query, act_keyval=act_keyval, act_output=act_output, act_gate=act_gate, act_up=act_up, act_down=act_down, act_norm_attn=act_norm_attn, act_norm_ffn=act_norm_ffn, action_embed=action_embed, prefix_cot=prefix_cot, suffix_cot=suffix_cot)


EPSILON = 1e-06

@jax.custom_vjp
def low(v):
    return lax.optimization_barrier(v.astype(jnp.bfloat16)).astype(jnp.float32)

@jax.custom_vjp
def low_back(v):
    return v

def low_keep(v):
    return (low(v), None)

def low_pass(kept, grad):
    return (grad,)

def back_keep(v):
    return (v, None)

def back_low(kept, grad):
    return (low(grad),)
low.defvjp(low_keep, low_pass)
low_back.defvjp(back_keep, back_low)

def both_round(value):
    return low_back(low(value))

def matmul(left, right):
    return jnp.dot(left, right, precision=lax.Precision.HIGHEST)

def rms_scale(values, gain):
    return values * lax.rsqrt(lax.optimization_barrier(jnp.mean(values * values, axis=-1, keepdims=True)) + EPSILON) * gain

def gelu_tanh(values):
    return jax.nn.gelu(values, approximate=True)

def feed_forward(resid, gain, w_gate, w_up, w_down):
    normed = low(rms_scale(resid, gain))
    gate = low_back(matmul(normed, w_gate))
    upward = low_back(matmul(normed, w_up))
    hidden = low(gelu_tanh(gate) * upward)
    return resid + low_back(matmul(hidden, w_down))

def one_item(weights, prefix_x, suffix_x, length, actions):
    pre_query, pre_keyval, pre_output, pre_gate, pre_up, pre_down, pre_norm_attn, pre_norm_ffn, act_query, act_keyval, act_output, act_gate, act_up, act_down, act_norm_attn, act_norm_ffn, action_embed = weights
    embedded = matmul(actions, action_embed)
    suffix_x = suffix_x + jnp.concatenate([jnp.zeros((1, DA), jnp.float32), embedded], axis=0)
    normed_pre = low(rms_scale(prefix_x, pre_norm_attn))
    normed_act = low(rms_scale(suffix_x, act_norm_attn))
    queries = both_round(jnp.concatenate([matmul(normed_pre, pre_query), matmul(normed_act, act_query)], axis=0))
    keyval = both_round(jnp.concatenate([matmul(normed_pre, pre_keyval), matmul(normed_act, act_keyval)], axis=0))
    seq_total = PREFIX + SUFFIX
    queries = queries.reshape(seq_total, HEADS, HD)
    keys = keyval[:, :HD]
    values = keyval[:, HD:]
    scale = HD ** (-0.5)
    scores = low_back(jnp.einsum('qhd,kd->hqk', queries, keys, precision=lax.Precision.HIGHEST) * scale)
    places = jnp.arange(seq_total)
    blocks = jnp.where(places < PREFIX, 0, jnp.where(places == PREFIX, 1, 2))
    key_live = (places < PREFIX) & (places < length)
    later = (places[:, None] >= PREFIX) & (places[None, :] >= PREFIX) & (blocks[None, :] <= blocks[:, None])
    allowed = key_live[None, :] | later
    masked = jnp.where(allowed[None], scores, -1e+30)
    top = lax.optimization_barrier(jnp.max(masked, axis=-1, keepdims=True))
    expo = jnp.exp(masked - top)
    probs = expo / lax.optimization_barrier(jnp.sum(expo, axis=-1, keepdims=True))
    attended = both_round(jnp.einsum('hqk,kd->qhd', low(probs), values, precision=lax.Precision.HIGHEST))
    attended = attended.reshape(seq_total, HEADS * HD)
    prefix_x = prefix_x + low_back(matmul(attended[:PREFIX], pre_output))
    suffix_x = suffix_x + low_back(matmul(attended[PREFIX:], act_output))
    return (feed_forward(prefix_x, pre_norm_ffn, pre_gate, pre_up, pre_down), feed_forward(suffix_x, act_norm_ffn, act_gate, act_up, act_down))

def reference(prefix_in, suffix_in, noisy_actions, prefix_len, action_live, pre_query, pre_keyval, pre_output, pre_gate, pre_up, pre_down, pre_norm_attn, pre_norm_ffn, act_query, act_keyval, act_output, act_gate, act_up, act_down, act_norm_attn, act_norm_ffn, action_embed, prefix_cot, suffix_cot):
    weights = tuple((w.astype(jnp.float32) for w in (pre_query, pre_keyval, pre_output, pre_gate, pre_up, pre_down, pre_norm_attn, pre_norm_ffn, act_query, act_keyval, act_output, act_gate, act_up, act_down, act_norm_attn, act_norm_ffn, action_embed)))
    inputs = (prefix_in.astype(jnp.float32), suffix_in.astype(jnp.float32))
    actions = jnp.where(action_live[:, None, :] == 1, noisy_actions.astype(jnp.float32), 0.0)

    def forward(inputs, weights):

        def run(pieces):
            return one_item(weights, pieces[0], pieces[1], pieces[2], pieces[3])
        return lax.map(jax.checkpoint(run), (inputs[0], inputs[1], prefix_len, actions))
    outputs, pull = jax.vjp(forward, inputs, weights)
    input_grads, weight_grads = pull((prefix_cot.astype(jnp.float32), suffix_cot.astype(jnp.float32)))
    g_pre_query, g_pre_keyval, g_pre_output, g_pre_gate, g_pre_up, g_pre_down, g_pre_norm_attn, g_pre_norm_ffn, g_act_query, g_act_keyval, g_act_output, g_act_gate, g_act_up, g_act_down, g_act_norm_attn, g_act_norm_ffn, g_action_embed = weight_grads
    return (outputs[0].astype(jnp.bfloat16), outputs[1].astype(jnp.bfloat16), input_grads[0], input_grads[1], g_pre_query, g_pre_keyval, g_pre_output, g_pre_gate, g_pre_up, g_pre_down, g_pre_norm_attn, g_pre_norm_ffn, g_act_query, g_act_keyval, g_act_output, g_act_gate, g_act_up, g_act_down, g_act_norm_attn, g_act_norm_ffn, g_action_embed)
```

```python
import functools

import jax
import jax.numpy as jnp
from jax import lax
from jax.sharding import PartitionSpec as P

HD = 256
EPSILON = 1e-06
PAD = 64
F32 = jnp.float32
BF16 = jnp.bfloat16


def rms_scale(values, gain):
    return values * lax.rsqrt(jnp.mean(values * values, axis=-1, keepdims=True) + EPSILON) * gain


def gelu_tanh(values):
    return jax.nn.gelu(values, approximate=True)


def geglu(gate, upward):
    return gelu_tanh(gate) * upward


def project(left, right):
    return jnp.dot(left, right, preferred_element_type=F32)


def project_back(left, right):
    return lax.dot_general(left, right, (((1,), (1,)), ((), ())), preferred_element_type=F32)


def outer_sum(left, right):
    return lax.dot_general(left, right, (((0,), (0,)), ((), ())), preferred_element_type=F32)


def norm_back(values, gain, cotangent):
    return jax.vjp(rms_scale, values, gain.astype(F32))[1](cotangent)


def attend(queries, keys, values, allowed, scale):
    scores = jnp.einsum("bqhe,bke->bhqk", queries, keys, preferred_element_type=F32) * scale
    masked = jnp.where(allowed[:, None], scores, -1e30)
    expo = jnp.exp(masked - jnp.max(masked, axis=-1, keepdims=True))
    probs = expo / jnp.sum(expo, axis=-1, keepdims=True)
    attended = jnp.einsum(
        "bhqk,bke->bqhe", probs.astype(BF16), values, preferred_element_type=F32
    )
    return attended.astype(BF16), probs


def attend_back(queries, keys, values, probs, grad_att, scale):
    grad_probs = jnp.einsum("bqhe,bke->bhqk", grad_att, values, preferred_element_type=F32)
    delta = jnp.sum(probs * grad_probs, axis=-1, keepdims=True)
    grad_scores = (probs * (grad_probs - delta)).astype(BF16)
    grad_queries = jnp.einsum("bhqk,bke->bqhe", grad_scores, keys, preferred_element_type=F32)
    grad_keys = jnp.einsum("bhqk,bqhe->bke", grad_scores, queries, preferred_element_type=F32)
    grad_values = jnp.einsum(
        "bhqk,bqhe->bke", probs.astype(BF16), grad_att, preferred_element_type=F32
    )
    return grad_queries * scale, grad_keys * scale, grad_values


def swap(value, axis, size, mask):
    return lax.ppermute(value, axis, [(i, i ^ mask) for i in range(size)])


def column_blocks(value, count):
    width = value.shape[1] // count
    return [value[:, i * width : (i + 1) * width] for i in range(count)]


def halves_down(value, axis):
    other = value.ndim - 1 if axis == value.ndim - 2 else value.ndim - 2
    size = value.shape[axis] // 2
    first = lax.slice_in_dim(value, 0, size, axis=axis)
    second = lax.slice_in_dim(value, size, 2 * size, axis=axis)
    return jnp.concatenate([first, second], axis=other)


def after(*values):
    return lax.optimization_barrier(values)


def own_first(value, dp, group):
    blocks = column_blocks(value, 2 * dp)
    even, odd = blocks[0::2], blocks[1::2]
    own = [jnp.where(group == 0, a, b) for a, b in zip(even, odd)]
    other = [jnp.where(group == 0, b, a) for a, b in zip(even, odd)]
    return jnp.concatenate(own + other, axis=1)


def own_first_undo(value, dp, group):
    blocks = column_blocks(value, 2 * dp)
    own, other = blocks[:dp], blocks[dp:]
    out = []
    for a, b in zip(own, other):
        out += [jnp.where(group == 0, a, b), jnp.where(group == 0, b, a)]
    return jnp.concatenate(out, axis=1)


class Rows:
    def __init__(self, part, suf_part, dp, core, x_index):
        self.part, self.dp, self.core, self.x_index = part, dp, core, x_index
        self.suf_part = suf_part
        self.size = part + suf_part // 2

    def pack(self, pre, suf):
        return jnp.concatenate([pre, halves_down(suf, 0)], axis=0)

    def unpack(self, value):
        return value[: self.part], halves_down(value[self.part :], 1)

    def tp_sum(self, pre, suf):
        width = pre.shape[1]
        pre = pre.astype(BF16).reshape(2, 2, self.part, width)
        suf = halves_down(suf.astype(BF16).reshape(4, self.suf_part, -1), 1)
        suf = suf.reshape(2, 2, -1, width)

        def pick(index, axis, *values):
            return jnp.concatenate(
                [lax.dynamic_index_in_dim(v, index, axis, keepdims=False) for v in values],
                axis=-2,
            )

        got = swap(pick(1 - self.core, 1, pre, suf), "tp", 4, 1)
        pair = pick(self.core, 1, pre, suf).astype(F32) + got.astype(F32)
        got = swap(pick(1 - self.x_index, 0, pair).astype(BF16), "tp", 4, 2)
        return self.unpack(pick(self.x_index, 0, pair) + got.astype(F32))

    def tp_gather(self, block):
        other = swap(block, "tp", 4, 2)
        low = jnp.where(self.x_index == 0, block, other)
        high = jnp.where(self.x_index == 0, other, block)
        pair = jnp.stack([low, high])
        got = swap(pair, "tp", 4, 1)
        even = jnp.where(self.core == 0, pair, got)
        odd = jnp.where(self.core == 0, got, pair)
        blocks = [even[0], odd[0], even[1], odd[1]]
        pre = jnp.concatenate([b[: self.part] for b in blocks], axis=0)
        suf = jnp.concatenate([halves_down(b[self.part :], 1) for b in blocks], axis=0)
        return pre, suf

    def pieces(self, value):
        n = value.shape[0] // self.size
        pre = [value[i * self.size : i * self.size + self.part] for i in range(n)]
        suf = [
            halves_down(value[i * self.size + self.part : (i + 1) * self.size], 1)
            for i in range(n)
        ]
        return pre, suf

    def spread(self, block, far):
        pair = jnp.concatenate([block, far], axis=0)
        got = swap(pair, "tp", 4, 1)
        first, second = self.pieces(pair), self.pieces(got)
        return jnp.concatenate(first[0] + second[0], axis=0), jnp.concatenate(
            first[1] + second[1], axis=0
        )

    def halves(self, value):
        size = value.shape[-2] // 2
        first = lax.slice_in_dim(value, 0, size, axis=value.ndim - 2)
        return first, lax.slice_in_dim(value, size, 2 * size, axis=value.ndim - 2)

    def first(self, pre, suf):
        pre, suf = self.halves(pre), self.halves(suf)
        return (pre[0], suf[0]), jnp.concatenate([pre[1], suf[1]], axis=-2)

    def second(self, keep, got):
        half = keep[0].shape[-2]
        got_pre = lax.slice_in_dim(got, 0, half, axis=got.ndim - 2)
        got_suf = lax.slice_in_dim(got, half, got.shape[-2], axis=got.ndim - 2)
        pre = self.halves(keep[0].astype(F32) + got_pre.astype(F32))
        suf = self.halves(keep[1].astype(F32) + got_suf.astype(F32))
        send = jnp.concatenate([pre[1], suf[1]], axis=-2).astype(BF16)
        return jnp.concatenate([pre[0], suf[0]], axis=-2), send

    def third(self, keep, got):
        return keep + got.astype(F32)


def local(
    dp,
    prefix_in,
    suffix_in,
    noisy_actions,
    prefix_len,
    action_live,
    pre_query,
    pre_keyval,
    pre_output,
    pre_gate,
    pre_up,
    pre_down,
    pre_norm_attn,
    pre_norm_ffn,
    act_query,
    act_keyval,
    act_output,
    act_gate,
    act_up,
    act_down,
    act_norm_attn,
    act_norm_ffn,
    action_embed,
    prefix_cot,
    suffix_cot,
):
    shards = 2 * dp
    both = ("dp", "expert")
    group = lax.axis_index("expert")
    t_index = lax.axis_index("tp")
    core, x_index = lax.rem(t_index, 2), t_index // 2
    pre_items, half_rows, width = prefix_in.shape
    _, suf_len, act_width = suffix_in.shape
    rows = pre_items * half_rows
    part = rows // 4
    suf_part = PAD // 4
    pack = Rows(part, suf_part, dp, core, x_index)
    scale = HD ** (-0.5)
    d_slice, q_cols = pre_query.shape
    a_slice = act_query.shape[0]
    heads = q_cols // HD
    hid = pre_gate.shape[1] // dp
    hid_act = act_gate.shape[1] // dp

    def half_cols(value):
        return lax.dynamic_slice_in_dim(value, core * HD, HD, 1)

    w1 = q_cols + HD
    small = [pre_norm_attn, pre_norm_ffn, act_norm_attn, act_norm_ffn, action_embed.reshape(-1)]
    small = jnp.concatenate(small)
    small_rows = -(-small.shape[0] // (16 * w1)) * 16
    small = jnp.pad(small, (0, small_rows * w1 - small.shape[0])).reshape(small_rows, w1)
    packed_in = jnp.concatenate(
        [
            jnp.concatenate([pre_query, half_cols(pre_keyval)], axis=1),
            jnp.concatenate([act_query, half_cols(act_keyval)], axis=1),
            small,
        ],
        axis=0,
    )
    z_index = lax.axis_index("dp")
    in_z = [packed_in] + [swap(packed_in, "dp", dp, d) for d in range(1, dp)]
    in_far = [swap(block, "expert", 2, 1) for block in in_z]

    def columns_out(pre, act):
        act_blocks = halves_down(jnp.stack(column_blocks(act, dp)), 2)
        return jnp.concatenate([jnp.stack(column_blocks(pre, dp)), act_blocks], axis=2)

    def columns_in(moved, pre, act):
        halves = jnp.concatenate(moved, axis=0)
        w_pre = halves[:, :, :hid].reshape(width, hid)
        w_act = halves_down(halves[:, :, hid:], 1).reshape(act_width, hid_act)
        return w_pre, w_act

    def dp_move(value):
        return lax.all_to_all(value, "dp", 0, 0, tiled=True)

    gate_out = columns_out(pre_gate, act_gate)
    up_out = columns_out(pre_up, act_up)
    down_out = jnp.concatenate(
        [
            pre_down.reshape(dp, hid, d_slice),
            halves_down(act_down.reshape(dp, hid_act, a_slice), 1),
        ],
        axis=1,
    )
    packed_out = jnp.concatenate([pre_output, act_output], axis=1)

    def own_rows(value):
        return lax.dynamic_slice_in_dim(value, t_index * part, part, 0)

    def own_suffix(value):
        return lax.dynamic_slice_in_dim(value, t_index * suf_part, suf_part, 0)

    def pad_suffix(value):
        return jnp.pad(value, ((0, PAD - suf_len), (0, 0)))

    def own_block(pre, suf):
        return pack.pack(own_first(pre, dp, group), own_first(suf, dp, group))

    def undo_block(block):
        pre, suf = pack.unpack(block)
        return own_first_undo(pre, dp, group), own_first_undo(suf, dp, group)

    cot_mine = own_rows(prefix_cot.reshape(rows, width))
    cot_suf_mine = own_suffix(pad_suffix(suffix_cot[0]))
    cot_block = own_block(cot_mine, cot_suf_mine)

    *in_near, gate_out, up_out, down_out, packed_out, cot_block = after(
        *in_z, gate_out, up_out, down_out, packed_out, cot_block
    )
    full_out = lax.all_gather(packed_out, both, axis=0)
    gate_own = dp_move(gate_out)
    full_in = jnp.zeros((dp, 2) + packed_in.shape, BF16)
    for d in range(dp):
        z = jnp.bitwise_xor(z_index, d)
        full_in = lax.dynamic_update_slice(full_in, in_near[d][None, None], (z, group, 0, 0))
        full_in = lax.dynamic_update_slice(full_in, in_far[d][None, None], (z, 1 - group, 0, 0))
    full_in = full_in.reshape((shards,) + packed_in.shape)

    w_pq = full_in[:, :d_slice, :q_cols].reshape(width, q_cols)
    w_pkv = full_in[:, :d_slice, q_cols:].reshape(width, HD)
    w_aq = full_in[:, d_slice : d_slice + a_slice, :q_cols].reshape(act_width, q_cols)
    w_akv = full_in[:, d_slice : d_slice + a_slice, q_cols:].reshape(act_width, HD)
    rest = full_in[:, d_slice + a_slice :].reshape(shards, small_rows * w1)
    gains, at = [], 0
    for size in (d_slice, d_slice, a_slice, a_slice):
        gains.append(rest[:, at : at + size].reshape(1, shards * size).astype(F32))
        at += size
    gain_pa, gain_pf, gain_aa, gain_af = gains
    embed = rest[:, at : at + action_embed.size].reshape(-1, act_width)
    prefix_x = prefix_in.astype(F32).reshape(rows, width)
    chosen = jnp.where(
        action_live[0][None, :] == 1, noisy_actions[0], jnp.zeros_like(noisy_actions[0])
    )
    chosen = jnp.pad(chosen, ((1, PAD - suf_len), (0, 0)))
    suffix_x = pad_suffix(suffix_in[0].astype(F32)) + project(chosen, embed)
    normed_pre = rms_scale(prefix_x, gain_pa).astype(BF16)
    normed_suf = rms_scale(suffix_x, gain_aa).astype(BF16)
    kv_pre = project(normed_pre, w_pkv).astype(BF16)
    kv_pre = kv_pre.reshape(pre_items, half_rows, HD)
    kv_got = swap(kv_pre, "expert", 2, 1)
    kv_suf = project(normed_suf, w_akv).astype(BF16)
    queries_pre = project(normed_pre, w_pq).astype(BF16).reshape(pre_items, half_rows, heads, HD)
    queries_suf = project(normed_suf, w_aq).astype(BF16).reshape(1, PAD, heads, HD)
    queries_pre, queries_suf, kv_suf, kv_got = after(queries_pre, queries_suf, kv_suf, kv_got)
    kv_pre = jnp.concatenate([kv_pre, kv_got], axis=1)
    full_len = kv_pre.shape[1]
    kv_mine = jnp.concatenate([kv_pre.reshape(pre_items * full_len, HD), kv_suf], axis=0)
    kv_other = swap(kv_mine, "tp", 4, 1)
    keys = jnp.where(core == 0, kv_mine, kv_other)
    values = jnp.where(core == 0, kv_other, kv_mine)

    def split_keys(value):
        pre = value[: pre_items * full_len].reshape(pre_items, full_len, HD)
        own = lax.dynamic_index_in_dim(pre, group, 0, keepdims=True)
        return pre, jnp.concatenate([own, value[None, pre_items * full_len :]], axis=1)

    keys_pre, keys_suf = split_keys(keys)
    values_pre, values_suf = split_keys(values)
    place = jnp.arange(full_len)
    first = place < half_rows
    place = jnp.where(first, place + group * half_rows, place - half_rows + (1 - group) * half_rows)
    key_live = place[None, :] < prefix_len[:, None]
    pre_allowed = jnp.broadcast_to(key_live[:, None, :], (pre_items, half_rows, full_len))
    own_live = lax.dynamic_index_in_dim(key_live, group, 0, keepdims=True)
    blocks = jnp.minimum(jnp.arange(PAD), 1)
    later = (blocks[None, :] <= blocks[:, None]) & (jnp.arange(PAD) < suf_len)[None, :]
    suf_allowed = jnp.concatenate(
        [jnp.broadcast_to(own_live[:, None, :], (1, PAD, full_len)), later[None]], axis=2
    )
    att_pre, probs_pre = attend(queries_pre, keys_pre, values_pre, pre_allowed, scale)
    att_suf, probs_suf = attend(queries_suf, keys_suf, values_suf, suf_allowed, scale)
    att_pre = att_pre.reshape(rows, q_cols)
    att_suf = att_suf.reshape(PAD, q_cols)

    att_pre, att_suf, full_out = after(att_pre, att_suf, full_out)
    w_po = jnp.concatenate([full_out[i, :, :d_slice] for i in range(shards)], axis=1)
    w_ao = jnp.concatenate([full_out[i, :, d_slice:] for i in range(shards)], axis=1)
    x_mine = own_rows(prefix_x)
    xs_mine = own_suffix(suffix_x)
    branch, branch_suf = project(att_pre, w_po).astype(BF16), project(att_suf, w_ao).astype(BF16)
    branch, branch_suf, gate_own, up_out = after(branch, branch_suf, gate_own, up_out)
    gate_got = swap(gate_own, "expert", 2, 1)
    up_own = dp_move(up_out)
    branch, branch_suf = pack.tp_sum(branch, branch_suf)
    resid = x_mine + branch
    resid_suf = xs_mine + branch_suf
    normed_block = own_block(
        rms_scale(resid, gain_pf).astype(BF16), rms_scale(resid_suf, gain_af).astype(BF16)
    )

    normed_z = [normed_block] + [swap(normed_block, "dp", dp, d) for d in range(1, dp)]
    normed_chunks, normed_sufs, gates, ups = [], [], [], []
    for d in range(dp):
        pre, suf = pack.spread(normed_z[d], swap(normed_z[d], "tp", 4, 2))
        if d == 0:
            pre, suf, up_own = after(pre, suf, up_own)
            up_got = swap(up_own, "expert", 2, 1)
            pre, gate_got = after(pre, gate_got)
            w_pg, w_ag = columns_in((gate_own, gate_got), pre_gate, act_gate)
        normed_chunks.append(pre)
        normed_sufs.append(suf)
        gates.append((project(pre, w_pg), project(suf, w_ag)))
    normed_last, down_out = after(normed_z[-1], down_out)
    down_own = dp_move(down_out)
    gates[-1], up_got = after(gates[-1], up_got)
    w_pu, w_au = columns_in((up_own, up_got), pre_up, act_up)
    for d in range(dp):
        ups.append((project(normed_chunks[d], w_pu), project(normed_sufs[d], w_au)))
    cot_far = swap(cot_block, "tp", 4, 2)
    ups[0], cot_far = after(ups[0], cot_far)
    cot_chunks = [pack.spread(cot_block, cot_far)]
    ups[-1], down_own, cot_block = after(ups[-1], down_own, cot_block)
    down_got = swap(down_own, "expert", 2, 1)
    cot_z = [swap(cot_block, "dp", dp, d) for d in range(1, dp)]
    cot_chunks += [pack.spread(z, swap(z, "tp", 4, 2)) for z in cot_z]
    down = jnp.concatenate([down_own, down_got], axis=0)
    w_pd = jnp.concatenate([down[i, :hid] for i in range(shards)], axis=1)
    act_down_blocks = halves_down(down[:, hid:], 2)
    w_ad = jnp.concatenate([act_down_blocks[i] for i in range(shards)], axis=1)

    def inner(gate, upward, cot, w_d):
        hidden, pull = jax.vjp(geglu, gate, upward)
        gate_cot, up_cot = pull(project_back(cot, w_d))
        return hidden.astype(BF16), gate_cot.astype(BF16), up_cot.astype(BF16)

    def back(gate_cot, up_cot, w_g, w_u):
        return (project_back(gate_cot, w_g) + project_back(up_cot, w_u)).astype(BF16)

    inners, inners_suf, pairs, sent, homes = {}, {}, {}, {}, {}

    def partial_of(d):
        pre = back(*inners[d][1:], w_pg, w_pu)
        suf = back(*inners_suf[d][1:], w_ag, w_au)
        suf = halves_down(suf.reshape(4, suf_part, act_width), 1).reshape(-1, width)
        return pre, suf

    def inner_of(d, *ties):
        cot, cot_suf = cot_chunks[d]
        gate, gate_suf, upward, upward_suf, *ties = after(*gates[d], *ups[d], *ties)
        inners[d] = inner(gate, upward, cot, w_pd)
        inners_suf[d] = inner(gate_suf, upward_suf, cot_suf, w_ad)
        return ties

    order = list(range(1, dp)) + [0]
    inner_of(0)
    last = inners[0][0]
    for i, d in enumerate(order):
        if d > 0:
            inner_of(d, last)
        if i > 0:
            e = order[i - 1]
            *inners[d], pairs[e] = after(*inners[d], pairs[e])
            keep, got = pairs[e][0], pairs[e][1]
            keep, send = pack.second(keep, got)
            *inners[d], send = after(*inners[d], send)
            pairs[e] = keep, swap(send, "tp", 4, 2)
        pre, suf = partial_of(d)
        last = pre
        keep, send = pack.first(pre, suf)
        pairs[d] = keep, swap(send, "tp", 4, 1)
        if i > 1:
            e = order[i - 2]
            *pairs[d], keep, got = after(*pairs[d], *pairs[e])
            homes[e] = swap(pack.third(keep, got).astype(BF16), "dp", dp, e)
    hiddens = [inners[d][0] for d in range(dp)]
    hid_suf = [inners_suf[d][0] for d in range(dp)]
    *hiddens, last, keep, got = after(*hiddens, last, *pairs[0])
    keep, send = pack.second(keep, got)
    pairs[0] = keep, swap(send, "tp", 4, 2)
    *hiddens, send = after(*hiddens, send)
    hidden_all = jnp.concatenate(hiddens, axis=0)
    outs = project(hidden_all, w_pd).astype(BF16).reshape(dp, rows, width)
    outs_suf = project(jnp.concatenate(hid_suf, axis=0), w_ad).astype(BF16)
    outs_suf = outs_suf.reshape(dp * 4, suf_part, act_width)
    outs_suf = halves_down(outs_suf, 1).reshape(dp, -1, width)
    for e in order[-2:-1]:
        outs, keep, got = after(outs, *pairs[e])
        homes[e] = swap(pack.third(keep, got).astype(BF16), "dp", dp, e)
    outs_keep, outs_send = pack.first(outs, outs_suf)
    outs_got = swap(outs_send, "tp", 4, 1)

    normed_suf_all = jnp.concatenate(normed_sufs, axis=0)
    cot_suf_all = jnp.concatenate([c[1] for c in cot_chunks], axis=0)
    h_suf, g_suf, u_suf = (
        jnp.concatenate([inners_suf[d][i] for d in range(dp)], axis=0) for i in range(3)
    )
    chunked = dp > 4
    if not chunked:
        normed_all = jnp.concatenate(normed_chunks, axis=0)
        cot_all = jnp.concatenate([c[0] for c in cot_chunks], axis=0)

    def outer_chunks(left, right):
        return sum(outer_sum(a, b) for a, b in zip(left, right))

    def normed_outer(i):
        right = [inners[d][i] for d in range(dp)]
        if chunked:
            return outer_chunks(normed_chunks, right)
        return outer_sum(normed_all, jnp.concatenate(right, axis=0))

    def columns_back(pre, act):
        pre = pre.reshape(shards, d_slice, hid)
        act = halves_down(act.reshape(shards, a_slice, hid_act), 2)
        whole = jnp.concatenate([pre, act], axis=2)
        return whole[:dp], swap(whole[dp:], "expert", 2, 1)

    def both_sum(own, got):
        return (own.astype(F32) + got.astype(F32)).astype(BF16)

    def columns_end(whole):
        pre = jnp.concatenate([whole[i, :, :hid] for i in range(dp)], axis=1)
        act = halves_down(whole[:, :, hid:], 1)
        act = jnp.concatenate([act[i] for i in range(dp)], axis=1)
        return pre.astype(F32), act.astype(F32)

    gate_grad = columns_back(
        normed_outer(1).astype(BF16), outer_sum(normed_suf_all, g_suf).astype(BF16)
    )
    g0, keep, got = after(gate_grad[0], *pairs[0])
    gate_grad = g0, gate_grad[1]
    home = pack.third(keep, got)
    up_grad = columns_back(
        normed_outer(2).astype(BF16), outer_sum(normed_suf_all, u_suf).astype(BF16)
    )

    for d in range(1, dp):
        home = home + homes[d].astype(F32)
    mcot, mcot_suf = undo_block(home)
    mid_part, ffn_gain = norm_back(resid, gain_pf, mcot)
    mid_part_suf, ffn_gain_suf = norm_back(resid_suf, gain_af, mcot_suf)
    mid = cot_mine.astype(F32) + mid_part
    mid_suf = cot_suf_mine.astype(F32) + mid_part_suf
    mid_block, hidden_all, outs_got = after(
        pack.pack(mid, mid_suf).astype(BF16), hidden_all, outs_got
    )
    bcot, bcot_suf = pack.tp_gather(mid_block)
    if chunked:
        down_pre = outer_chunks(
            [hidden_all[d * rows : (d + 1) * rows] for d in range(dp)], [c[0] for c in cot_chunks]
        ).astype(BF16)
    else:
        down_pre = outer_sum(hidden_all, cot_all).astype(BF16)
    down_act = outer_sum(h_suf, cot_suf_all).astype(BF16)
    down_grad = jnp.concatenate(
        [
            jnp.stack(column_blocks(down_pre, shards)),
            halves_down(jnp.stack(column_blocks(down_act, shards)), 1),
        ],
        axis=1,
    )
    down_grad = down_grad[:dp], swap(down_grad[dp:], "expert", 2, 1)
    bcot, bcot_suf, gate_grad, outs_got = after(bcot, bcot_suf, gate_grad, outs_got)
    outs_keep, outs_send = pack.second(outs_keep, outs_got)
    outs_got = swap(outs_send, "tp", 4, 2)
    gate_grad = dp_move(both_sum(*gate_grad))
    acot_pre = project_back(bcot, w_po).astype(BF16).reshape(pre_items, half_rows, heads, HD)
    acot_suf = project_back(bcot_suf, w_ao).astype(BF16).reshape(1, PAD, heads, HD)
    qcot_pre, kcot_pre, vcot_pre = attend_back(
        queries_pre, keys_pre, values_pre, probs_pre, acot_pre, scale
    )
    qcot_suf, kcot_suf, vcot_suf = attend_back(
        queries_suf, keys_suf, values_suf, probs_suf, acot_suf, scale
    )

    def join(pre, suf):
        mine = lax.dynamic_index_in_dim(pre, group, 0, keepdims=True) + suf[:, :full_len]
        pre = lax.dynamic_update_slice_in_dim(pre, mine, group, 0)
        pre = pre.reshape(pre_items * full_len, HD)
        return jnp.concatenate([pre, suf[0, full_len:]], axis=0)

    kcot, vcot = join(kcot_pre, kcot_suf), join(vcot_pre, vcot_suf)
    got = swap(jnp.where(core == 0, vcot, kcot).astype(BF16), "tp", 4, 1)
    kvcot = jnp.where(core == 0, kcot, vcot) + got.astype(F32)
    kv_pre_cot = kvcot[: pre_items * full_len].reshape(pre_items, 2, half_rows, HD)
    got = swap(kv_pre_cot[:, 1].astype(BF16), "expert", 2, 1)
    kv_pre_cot = kv_pre_cot[:, 0] + got.astype(F32)
    kvcot = jnp.concatenate(
        [kv_pre_cot.reshape(rows, HD), kvcot[pre_items * full_len :]], axis=0
    )
    got = swap(kvcot.astype(BF16), "tp", 4, 2)
    kvcot = (kvcot + got.astype(F32)).astype(BF16)
    kvcot, gate_grad, up_grad, outs_got = after(kvcot, gate_grad, up_grad, outs_got)
    outs = pack.third(outs_keep, outs_got)
    outs = [outs[0]] + [swap(outs[d].astype(BF16), "dp", dp, d).astype(F32) for d in range(1, dp)]
    up_grad = dp_move(both_sum(*up_grad))
    key_half, key_own = kvcot[:rows], kvcot[rows:]
    qcot_pre = qcot_pre.astype(BF16).reshape(rows, q_cols)
    qcot_suf = qcot_suf.astype(BF16).reshape(PAD, q_cols)
    ncot = project_back(qcot_pre, w_pq) + 0.5 * project_back(key_half, w_pkv)
    ncot_suf = project_back(qcot_suf, w_aq) + 0.5 * project_back(key_own, w_akv)
    ncot, ncot_suf = pack.tp_sum(ncot, ncot_suf)
    in_part, attn_gain = norm_back(x_mine, gain_pa, ncot)
    in_part_suf, attn_gain_suf = norm_back(xs_mine, gain_aa, ncot_suf)
    grad_mine = mid + in_part
    grad_suf_mine = mid_suf + in_part_suf
    embed_w = lax.dot_general(
        own_suffix(chosen).astype(F32),
        grad_suf_mine,
        (((0,), (0,)), ((), ())),
        precision=lax.Precision.HIGHEST,
    )
    tail = jnp.concatenate(
        [
            attn_gain.reshape(shards, -1),
            ffn_gain.reshape(shards, -1),
            attn_gain_suf.reshape(shards, -1),
            ffn_gain_suf.reshape(shards, -1),
            embed_w.reshape(shards, -1),
        ],
        axis=1,
    )

    out_w = jnp.concatenate(
        [
            jnp.stack(column_blocks(outer_sum(att_pre, bcot).astype(BF16), shards)),
            jnp.stack(column_blocks(outer_sum(att_suf, bcot_suf).astype(BF16), shards)),
        ],
        axis=2,
    )
    in_w = jnp.concatenate(
        [
            jnp.concatenate(
                [
                    outer_sum(normed_pre, qcot_pre).astype(BF16).reshape(shards, d_slice, q_cols),
                    outer_sum(normed_pre, key_half).astype(BF16).reshape(shards, d_slice, HD),
                ],
                axis=2,
            ),
            jnp.concatenate(
                [
                    outer_sum(normed_suf, qcot_suf).astype(BF16).reshape(shards, a_slice, q_cols),
                    outer_sum(normed_suf, key_own).astype(BF16).reshape(shards, a_slice, HD),
                ],
                axis=2,
            ),
        ],
        axis=1,
    )

    def scatter_y(value):
        value = value.reshape((dp, 2) + value.shape[1:])
        send = lax.dynamic_index_in_dim(value, 1 - group, 1, keepdims=False)
        keep = lax.dynamic_index_in_dim(value, group, 1, keepdims=False)
        return keep, swap(send, "expert", 2, 1)

    def scatter_z(moved):
        return jnp.sum(dp_move(both_sum(*moved)).astype(F32), axis=0)

    out_w = scatter_y(out_w)
    in_w = scatter_y(in_w)
    in_w, up_grad, down_grad = after(in_w, up_grad, down_grad)
    down_grad = dp_move(both_sum(*down_grad))
    out_w = scatter_z(out_w)
    in_w = scatter_z(in_w)
    g_po, g_ao = out_w[:, :d_slice], out_w[:, d_slice:]
    g_pq, g_aq = in_w[:d_slice, :q_cols], in_w[d_slice:, :q_cols]
    kv_w = in_w[:, q_cols:].astype(BF16)
    kv_other = swap(kv_w, "tp", 4, 1).astype(F32)
    kv_w = kv_w.astype(F32)
    kv_w = jnp.concatenate(
        [jnp.where(core == 0, kv_w, kv_other), jnp.where(core == 0, kv_other, kv_w)], axis=1
    )
    g_pkv, g_akv = kv_w[:d_slice], kv_w[d_slice:]

    out_pre, out_suf = undo_block(sum(outs))
    out_block = pack.pack(resid + out_pre, resid_suf + out_suf).astype(BF16)
    out_pre, out_suf = pack.tp_gather(out_block)
    prefix_out = out_pre.reshape(pre_items, half_rows, width)
    suffix_out = out_suf[None, :suf_len]
    grad_pre, grad_suf = pack.tp_gather(pack.pack(grad_mine, grad_suf_mine).astype(BF16))
    prefix_grad = grad_pre.astype(F32).reshape(pre_items, half_rows, width)
    suffix_grad = grad_suf.astype(F32)[None, :suf_len]
    g_pg, g_ag = columns_end(gate_grad)
    g_pu, g_au = columns_end(up_grad)
    g_pd = down_grad[:, :hid].reshape(dp * hid, d_slice).astype(F32)
    g_ad = halves_down(down_grad[:, hid:], 2).reshape(dp * hid_act, a_slice).astype(F32)
    tail = jnp.broadcast_to(tail[:, None, None], (shards, 4, 1, tail.shape[1]))
    tail = tail.reshape(4 * shards, 1, -1)
    tail = lax.all_to_all(tail, ("dp", "expert", "tp"), 0, 0, tiled=True)
    tail = jnp.sum(tail, axis=0)[0]
    tails, at = [], 0
    for size in (d_slice, d_slice, a_slice, a_slice, action_embed.size):
        tails.append(tail[at : at + size])
        at += size
    g_gpa, g_gpf, g_gaa, g_gaf, g_embed = tails
    g_embed = g_embed.reshape(action_embed.shape)
    return (
        prefix_out,
        suffix_out,
        prefix_grad,
        suffix_grad,
        g_pq,
        g_pkv,
        g_po,
        g_pg,
        g_pu,
        g_pd,
        g_gpa,
        g_gpf,
        g_aq,
        g_akv,
        g_ao,
        g_ag,
        g_au,
        g_ad,
        g_gaa,
        g_gaf,
        g_embed,
    )


def solution(mesh):
    return jax.shard_map(
        functools.partial(local, mesh.shape["dp"]),
        mesh=mesh,
        in_specs=(
            P("dp", "expert", None),
            P(("dp", "expert"), None, None),
            P(("dp", "expert"), None, None),
            P("dp"),
            P(("dp", "expert"), None),
            P(("dp", "expert"), "tp"),
            P(("dp", "expert"), None),
            P("tp", ("dp", "expert")),
            P(("dp", "expert"), "tp"),
            P(("dp", "expert"), "tp"),
            P("tp", ("dp", "expert")),
            P(("dp", "expert")),
            P(("dp", "expert")),
            P(("dp", "expert"), "tp"),
            P(("dp", "expert"), None),
            P("tp", ("dp", "expert")),
            P(("dp", "expert"), "tp"),
            P(("dp", "expert"), "tp"),
            P("tp", ("dp", "expert")),
            P(("dp", "expert")),
            P(("dp", "expert")),
            P(("dp", "expert"), None),
            P("dp", "expert", None),
            P(("dp", "expert"), None, None),
        ),
        out_specs=(
            P("dp", "expert", None),
            P(("dp", "expert"), None, None),
            P("dp", "expert", None),
            P(("dp", "expert"), None, None),
            P(("dp", "expert"), "tp"),
            P(("dp", "expert"), None),
            P("tp", ("dp", "expert")),
            P(("dp", "expert"), "tp"),
            P(("dp", "expert"), "tp"),
            P("tp", ("dp", "expert")),
            P(("dp", "expert")),
            P(("dp", "expert")),
            P(("dp", "expert"), "tp"),
            P(("dp", "expert"), None),
            P("tp", ("dp", "expert")),
            P(("dp", "expert"), "tp"),
            P(("dp", "expert"), "tp"),
            P("tp", ("dp", "expert")),
            P(("dp", "expert")),
            P(("dp", "expert")),
            P(("dp", "expert"), None),
        ),
        check_vma=False,
    )
```

```python
import functools

import jax
import jax.numpy as jnp
from jax import lax
from jax.experimental import pallas as pl
from jax.experimental.pallas import tpu as pltpu
from jax.sharding import PartitionSpec as P

HD = 256
EPSILON = 1e-06
PAD = 64
F32 = jnp.float32
BF16 = jnp.bfloat16


def rms_scale(values, gain):
    return values * lax.rsqrt(jnp.mean(values * values, axis=-1, keepdims=True) + EPSILON) * gain


def gelu_tanh(values):
    return jax.nn.gelu(values, approximate=True)


def geglu(gate, upward):
    return gelu_tanh(gate) * upward


def project(left, right):
    return jnp.dot(left, right, preferred_element_type=F32)


def project_back(left, right):
    return lax.dot_general(left, right, (((1,), (1,)), ((), ())), preferred_element_type=F32)


def outer_sum(left, right):
    return lax.dot_general(left, right, (((0,), (0,)), ((), ())), preferred_element_type=F32)


def norm_back(values, gain, cotangent):
    return jax.vjp(rms_scale, values, gain.astype(F32))[1](cotangent)


MIB = 1024 * 1024


def key_mask(shape, start, length, group, half_rows):
    place = lax.broadcasted_iota(jnp.int32, shape, 1)
    own = jnp.where(place < half_rows, group, 1 - group) * half_rows
    place = jnp.where(place < half_rows, place, place - half_rows) + own
    return place < length


def softmax_parts(scores):
    top = functools.reduce(jnp.maximum, [jnp.max(s, axis=1, keepdims=True) for s in scores])
    expo = [jnp.exp(s - top) for s in scores]
    denom = sum(jnp.sum(e, axis=1, keepdims=True) for e in expo)
    return [e / denom for e in expo]


def suffix_scores(q, keys, own_keys, live, later, scale):
    first = jnp.where(live, project_back(q, keys) * scale, -1e30)
    second = jnp.where(later, project_back(q, own_keys) * scale, -1e30)
    return softmax_parts([first, second])


def suffix_masks(suf_len, full, length, group, half_rows):
    live = key_mask((PAD, full), 0, length, group, half_rows)
    row = lax.broadcasted_iota(jnp.int32, (PAD, PAD), 0)
    column = lax.broadcasted_iota(jnp.int32, (PAD, PAD), 1)
    later = ((column == 0) | (row > 0)) & (column < suf_len)
    return live, later


def attend_kernel(items, heads, suf_len, info, q, qs, k, v, att, att_suf):
    scale = HD ** (-0.5)
    rows = q.shape[0] // items
    full = (k.shape[0] - PAD) // items
    group = info[0]
    for i in range(items):
        live = key_mask((rows, full), 0, info[1 + i], group, rows)
        for h in range(heads):
            at, keys = (slice(i * rows, (i + 1) * rows), slice(h * HD, (h + 1) * HD)), slice(i * full, (i + 1) * full)
            scores = jnp.where(live, project_back(q[at], k[keys]) * scale, -1e30)
            (probs,) = softmax_parts([scores])
            att[at] = project(probs.astype(BF16), v[keys]).astype(BF16)
    live, later = suffix_masks(suf_len, full, info[1 + items], group, rows)
    start = pl.multiple_of(group * full, full)
    keys, values = k[pl.ds(start, full)], v[pl.ds(start, full)]
    own_keys, own_values = k[items * full :], v[items * full :]
    for h in range(heads):
        at = (slice(None), slice(h * HD, (h + 1) * HD))
        first, second = suffix_scores(qs[at], keys, own_keys, live, later, scale)
        total = project(first.astype(BF16), values) + project(second.astype(BF16), own_values)
        att_suf[at] = total.astype(BF16)


def attend_back_kernel(items, heads, suf_len, info, q, qs, k, v, cot, cot_suf, qcot, qcot_suf, kcot, vcot):
    scale = HD ** (-0.5)
    rows = q.shape[0] // items
    full = (k.shape[0] - PAD) // items
    group = info[0]
    for i in range(items):
        live = key_mask((rows, full), 0, info[1 + i], group, rows)
        for h in range(heads):
            at, keys = (slice(i * rows, (i + 1) * rows), slice(h * HD, (h + 1) * HD)), slice(i * full, (i + 1) * full)
            scores = jnp.where(live, project_back(q[at], k[keys]) * scale, -1e30)
            (probs,) = softmax_parts([scores])
            grad = project_back(cot[at], v[keys])
            delta = jnp.sum(probs * grad, axis=1, keepdims=True)
            inner = (probs * (grad - delta)).astype(BF16)
            qcot[at] = (project(inner, k[keys]) * scale).astype(BF16)
            kterm = outer_sum(inner, q[at]) * scale
            vterm = outer_sum(probs.astype(BF16), cot[at])
            if h == 0:
                kcot[keys], vcot[keys] = kterm, vterm
            else:
                kcot[keys] += kterm
                vcot[keys] += vterm
    live, later = suffix_masks(suf_len, full, info[1 + items], group, rows)
    start = pl.multiple_of(group * full, full)
    own = slice(items * full, items * full + PAD)
    place = pl.ds(start, full)
    for h in range(heads):
        at = (slice(None), slice(h * HD, (h + 1) * HD))
        first, second = suffix_scores(qs[at], k[place], k[own], live, later, scale)
        grads = project_back(cot_suf[at], v[place]), project_back(cot_suf[at], v[own])
        delta = sum(jnp.sum(p * g, axis=1, keepdims=True) for p, g in zip((first, second), grads))
        inners = [(p * (g - delta)).astype(BF16) for p, g in zip((first, second), grads)]
        total = project(inners[0], k[place]) + project(inners[1], k[own])
        qcot_suf[at] = (total * scale).astype(BF16)
        kcot[place] += outer_sum(inners[0], qs[at]) * scale
        vcot[place] += outer_sum(first.astype(BF16), cot_suf[at])
        kterm = outer_sum(inners[1], qs[at]) * scale
        vterm = outer_sum(second.astype(BF16), cot_suf[at])
        if h == 0:
            kcot[own], vcot[own] = kterm, vterm
        else:
            kcot[own] += kterm
            vcot[own] += vterm


def attention_call(kernel, name, out_shape, items, heads, suf_len, info, *arrays):
    spec = pl.BlockSpec(memory_space=pltpu.VMEM)
    return pl.pallas_call(
        functools.partial(kernel, items, heads, suf_len),
        in_specs=[pl.BlockSpec(memory_space=pltpu.SMEM)] + [spec] * len(arrays),
        out_specs=[spec] * len(out_shape),
        out_shape=out_shape,
        compiler_params=pltpu.CompilerParams(vmem_limit_bytes=32 * MIB),
        name=name,
    )(info, *arrays)


def attend(info, q, qs, k, v, items, suf_len):
    shape = [jax.ShapeDtypeStruct(q.shape, BF16), jax.ShapeDtypeStruct(qs.shape, BF16)]
    heads = q.shape[1] // HD
    return attention_call(attend_kernel, "attend", shape, items, heads, suf_len, info, q, qs, k, v)


def attend_back(info, q, qs, k, v, cot, cot_suf, items, suf_len):
    shape = [jax.ShapeDtypeStruct(a.shape, t) for a, t in ((q, BF16), (qs, BF16), (k, F32), (v, F32))]
    heads = q.shape[1] // HD
    return attention_call(
        attend_back_kernel, "attend_back", shape, items, heads, suf_len, info, q, qs, k, v, cot, cot_suf
    )


def swap(value, axis, size, mask):
    return lax.ppermute(value, axis, [(i, i ^ mask) for i in range(size)])


def column_blocks(value, count):
    width = value.shape[1] // count
    return [value[:, i * width : (i + 1) * width] for i in range(count)]


def halves_down(value, axis):
    other = value.ndim - 1 if axis == value.ndim - 2 else value.ndim - 2
    size = value.shape[axis] // 2
    first = lax.slice_in_dim(value, 0, size, axis=axis)
    second = lax.slice_in_dim(value, size, 2 * size, axis=axis)
    return jnp.concatenate([first, second], axis=other)


def after(*values):
    return lax.optimization_barrier(values)


def own_first(value, dp, group):
    width = value.shape[1] // (2 * dp)
    zero = jnp.zeros((), value.dtype)
    right = lax.pad(value, zero, ((0, 0, 0), (-width, width, 0)))
    left = lax.pad(value, zero, ((0, 0, 0), (width, -width, 0)))
    block = lax.broadcasted_iota(jnp.int32, value.shape, 1) // width
    return jnp.where(group == 0, value, jnp.where(block % 2 == 0, right, left))


class Rows:
    def __init__(self, part, suf_part, width, act_width, core, x_index):
        self.part, self.suf_part, self.core, self.x_index = part, suf_part, core, x_index
        self.width, self.act_width = width, act_width

    def join(self, pre, suf):
        zero = jnp.zeros((), suf.dtype)
        suf = lax.pad(suf, zero, ((0, 0, 0), (0, self.width - self.act_width, 0)))
        pre = pre.reshape(-1, self.part, self.width)
        return jnp.concatenate([pre, suf.reshape(-1, self.suf_part, self.width)], axis=1)

    def split(self, blocks):
        pre = blocks[:, : self.part].reshape(-1, self.width)
        return pre, blocks[:, self.part :, : self.act_width].reshape(-1, self.act_width)

    def tp_sum(self, pre, suf):
        whole = self.join(pre.astype(BF16), suf.astype(BF16))
        whole = whole.reshape(2, 2, -1, self.width)

        def pick(value, index, axis):
            return lax.dynamic_index_in_dim(value, index, axis, keepdims=False)

        got = swap(pick(whole, 1 - self.core, 1), "tp", 4, 1)
        pair = pick(whole, self.core, 1).astype(F32) + got.astype(F32)
        got = swap(pick(pair, 1 - self.x_index, 0).astype(BF16), "tp", 4, 2)
        return self.split((pick(pair, self.x_index, 0) + got.astype(F32))[None])

    def tp_gather(self, block):
        other = swap(block, "tp", 4, 2)
        low = jnp.where(self.x_index == 0, block, other)
        high = jnp.where(self.x_index == 0, other, block)
        pair = jnp.concatenate([low, high], axis=0)
        got = swap(pair, "tp", 4, 1)
        even = jnp.where(self.core == 0, pair, got)
        odd = jnp.where(self.core == 0, got, pair)
        return self.split(jnp.stack([even, odd], axis=1).reshape(4, -1, self.width))

    def spread(self, block, far):
        pair = jnp.concatenate([block, far], axis=0)
        return self.split(jnp.concatenate([pair, swap(pair, "tp", 4, 1)], axis=0))

    def first(self, pre, suf):
        whole = self.join(pre, suf).reshape(-1, 4, self.part + self.suf_part, self.width)
        return whole[:, :2], whole[:, 2:]

    def second(self, keep, got):
        pair = keep.astype(F32) + got.astype(F32)
        return pair[:, 0], pair[:, 1].astype(BF16)

    def third(self, keep, got):
        return keep + got.astype(F32)


def local(
    dp,
    prefix_in,
    suffix_in,
    noisy_actions,
    prefix_len,
    action_live,
    pre_query,
    pre_keyval,
    pre_output,
    pre_gate,
    pre_up,
    pre_down,
    pre_norm_attn,
    pre_norm_ffn,
    act_query,
    act_keyval,
    act_output,
    act_gate,
    act_up,
    act_down,
    act_norm_attn,
    act_norm_ffn,
    action_embed,
    prefix_cot,
    suffix_cot,
):
    shards = 2 * dp
    both = ("dp", "expert")
    group = lax.axis_index("expert")
    t_index = lax.axis_index("tp")
    core, x_index = lax.rem(t_index, 2), t_index // 2
    pre_items, half_rows, width = prefix_in.shape
    _, suf_len, act_width = suffix_in.shape
    rows = pre_items * half_rows
    part = rows // 4
    suf_part = PAD // 4
    pack = Rows(part, suf_part, width, act_width, core, x_index)
    d_slice, q_cols = pre_query.shape
    a_slice = act_query.shape[0]
    hid = pre_gate.shape[1] // dp
    hid_act = act_gate.shape[1] // dp

    def half_cols(value):
        return lax.dynamic_slice_in_dim(value, core * HD, HD, 1)

    w1 = q_cols + HD
    small = [pre_norm_attn, pre_norm_ffn, act_norm_attn, act_norm_ffn, action_embed.reshape(-1)]
    small = jnp.concatenate(small)
    small_rows = -(-small.shape[0] // (16 * w1)) * 16
    small = jnp.pad(small, (0, small_rows * w1 - small.shape[0])).reshape(small_rows, w1)
    packed_in = jnp.concatenate(
        [
            jnp.concatenate([pre_query, half_cols(pre_keyval)], axis=1),
            jnp.concatenate([act_query, half_cols(act_keyval)], axis=1),
            small,
        ],
        axis=0,
    )
    z_index = lax.axis_index("dp")
    in_z = [packed_in] + [swap(packed_in, "dp", dp, d) for d in range(1, dp)]
    in_far = [swap(packed_in, "expert", 2, 1)]

    def columns_out(pre, act):
        act_blocks = halves_down(jnp.stack(column_blocks(act, dp)), 2)
        return jnp.concatenate([jnp.stack(column_blocks(pre, dp)), act_blocks], axis=2)

    def columns_in(moved, pre, act):
        halves = jnp.stack(moved, axis=1)
        w_pre = halves[..., :hid].reshape(width, hid)
        w_act = halves_down(halves[..., hid:], 2).reshape(act_width, hid_act)
        return w_pre, w_act

    def dp_move(value):
        return lax.all_to_all(value, "dp", 0, 0, tiled=True)

    gate_out = columns_out(pre_gate, act_gate)
    up_out = columns_out(pre_up, act_up)
    down_out = jnp.concatenate(
        [
            pre_down.reshape(dp, hid, d_slice),
            halves_down(act_down.reshape(dp, hid_act, a_slice), 1),
        ],
        axis=1,
    )
    packed_out = jnp.concatenate([pre_output, act_output], axis=1)

    def own_rows(value):
        return lax.dynamic_slice_in_dim(value, t_index * part, part, 0)

    def own_suffix(value):
        return lax.dynamic_slice_in_dim(value, t_index * suf_part, suf_part, 0)

    def pad_suffix(value):
        return jnp.pad(value, ((0, PAD - suf_len), (0, 0)))

    def own_block(pre, suf):
        return pack.join(own_first(pre, dp, group), own_first(suf, dp, group))

    def undo_block(block):
        pre, suf = pack.split(block)
        return own_first(pre, dp, group), own_first(suf, dp, group)

    cot_mine = own_rows(prefix_cot.reshape(rows, width))
    cot_suf_mine = own_suffix(pad_suffix(suffix_cot[0]))
    cot_block = own_block(cot_mine, cot_suf_mine)

    gate_own = dp_move(gate_out)
    *in_z, gate_own, packed_out = after(*in_z, gate_own, packed_out)
    in_far += [swap(block, "expert", 2, 1) for block in in_z[1:]]
    full_out = lax.all_gather(packed_out, both, axis=0)
    *in_far, up_out = after(*in_far, up_out)
    up_own = dp_move(up_out)
    full_in = jnp.zeros((dp, 2) + packed_in.shape, BF16)
    for d in range(dp):
        z = jnp.bitwise_xor(z_index, d)
        full_in = lax.dynamic_update_slice(full_in, in_z[d][None, None], (z, group, 0, 0))
        full_in = lax.dynamic_update_slice(full_in, in_far[d][None, None], (z, 1 - group, 0, 0))
    full_in = full_in.reshape((shards,) + packed_in.shape)

    w_pq = full_in[:, :d_slice, :q_cols].reshape(width, q_cols)
    w_pkv = full_in[:, :d_slice, q_cols:].reshape(width, HD)
    w_aq = full_in[:, d_slice : d_slice + a_slice, :q_cols].reshape(act_width, q_cols)
    w_akv = full_in[:, d_slice : d_slice + a_slice, q_cols:].reshape(act_width, HD)
    rest = full_in[:, d_slice + a_slice :].reshape(shards, small_rows * w1)
    gains, at = [], 0
    for size in (d_slice, d_slice, a_slice, a_slice):
        gains.append(rest[:, at : at + size].reshape(1, shards * size).astype(F32))
        at += size
    gain_pa, gain_pf, gain_aa, gain_af = gains
    embed = rest[:, at : at + action_embed.size].reshape(-1, act_width)
    prefix_x = prefix_in.astype(F32).reshape(rows, width)
    chosen = jnp.where(
        action_live[0][None, :] == 1, noisy_actions[0], jnp.zeros_like(noisy_actions[0])
    )
    chosen = jnp.pad(chosen, ((1, PAD - suf_len), (0, 0)))
    suffix_x = pad_suffix(suffix_in[0].astype(F32)) + project(chosen, embed)
    normed_pre = rms_scale(prefix_x, gain_pa).astype(BF16)
    normed_suf = rms_scale(suffix_x, gain_aa).astype(BF16)
    kv_pre = project(normed_pre, w_pkv).astype(BF16)
    kv_pre = kv_pre.reshape(pre_items, half_rows, HD)
    kv_got = swap(kv_pre, "expert", 2, 1)
    kv_suf = project(normed_suf, w_akv).astype(BF16)
    queries_pre = project(normed_pre, w_pq).astype(BF16)
    queries_suf = project(normed_suf, w_aq).astype(BF16)
    queries_pre, queries_suf, kv_suf, kv_got, gate_own = after(
        queries_pre, queries_suf, kv_suf, kv_got, gate_own
    )
    gate_got = swap(gate_own, "expert", 2, 1)
    kv_pre = jnp.concatenate([kv_pre, kv_got], axis=1)
    full_len = kv_pre.shape[1]
    kv_mine = jnp.concatenate([kv_pre.reshape(pre_items * full_len, HD), kv_suf], axis=0)
    kv_other = swap(kv_mine, "tp", 4, 1)
    keys = jnp.where(core == 0, kv_mine, kv_other)
    values = jnp.where(core == 0, kv_other, kv_mine)

    own_len = lax.dynamic_slice_in_dim(prefix_len, group, 1)
    info = jnp.concatenate([group.reshape(1).astype(jnp.int32), prefix_len, own_len])
    att_pre, att_suf = attend(info, queries_pre, queries_suf, keys, values, pre_items, suf_len)
    att_pre, att_suf, full_out = after(att_pre, att_suf, full_out)
    w_po = jnp.concatenate([full_out[i, :, :d_slice] for i in range(shards)], axis=1)
    w_ao = jnp.concatenate([full_out[i, :, d_slice:] for i in range(shards)], axis=1)
    x_mine = own_rows(prefix_in.reshape(rows, width)).astype(F32)
    xs_mine = own_suffix(suffix_x)
    branch = pack.tp_sum(project(att_pre, w_po), project(att_suf, w_ao))
    branch, branch_suf = branch
    resid = x_mine + branch
    resid_suf = xs_mine + branch_suf
    normed_block = own_block(
        rms_scale(resid, gain_pf).astype(BF16), rms_scale(resid_suf, gain_af).astype(BF16)
    )

    normed_far = swap(normed_block, "tp", 4, 2)
    normed_z = [normed_block] + [swap(normed_block, "dp", dp, d) for d in range(1, dp)]
    normed_far, up_own, gate_got = after(normed_far, up_own, gate_got)
    up_got = swap(up_own, "expert", 2, 1)
    *normed_z, down_out = after(*normed_z, down_out)
    down_own = dp_move(down_out)
    w_pg, w_ag = columns_in((gate_own, gate_got), pre_gate, act_gate)
    normed_chunks, gates, inner_terms = [], [], []

    def gelu_terms(gate):
        value, pull = jax.vjp(gelu_tanh, gate)
        return value, pull(jnp.ones_like(gate))[0]

    def scale_terms(gate, upward):
        value, slope = gate
        return (value * upward).astype(BF16), upward * slope, value

    for d in range(dp):
        far = normed_far if d == 0 else swap(normed_z[d], "tp", 4, 2)
        pre, suf = pack.spread(normed_z[d], far)
        if d > 0:
            pre, suf, *gates[-1] = after(pre, suf, *gates[-1])
        normed_chunks.append((pre, suf))
        gates.append((gelu_terms(project(pre, w_pg)), gelu_terms(project(suf, w_ag))))
    gates[-1], up_got = after(gates[-1], up_got)
    w_pu, w_au = columns_in((up_own, up_got), pre_up, act_up)
    for d in range(dp):
        pre, suf = normed_chunks[d]
        terms = scale_terms(gates[d][0], project(pre, w_pu))
        terms += scale_terms(gates[d][1], project(suf, w_au))
        inner_terms.append(after(*terms))
    cot_far = swap(cot_block, "tp", 4, 2)
    inner_terms[0], cot_far = after(inner_terms[0], cot_far)
    cot_chunks = [pack.spread(cot_block, cot_far)]
    inner_terms[0], cot_block, down_own = after(inner_terms[0], cot_block, down_own)
    down_got = swap(down_own, "expert", 2, 1)
    cot_z = [swap(cot_block, "dp", dp, d) for d in range(1, dp)]
    cot_chunks += [pack.spread(z, swap(z, "tp", 4, 2)) for z in cot_z]
    down = jnp.stack([down_own, down_got], axis=1).reshape(shards, hid + hid_act // 2, d_slice)
    w_pd = jnp.concatenate([down[i, :hid] for i in range(shards)], axis=1)
    act_down_blocks = halves_down(down[:, hid:], 2)
    w_ad = jnp.concatenate([act_down_blocks[i] for i in range(shards)], axis=1)

    def inner(terms, cot, w_d):
        hidden, gate_term, up_term = terms
        grad = project_back(cot, w_d)
        return hidden, (grad * gate_term).astype(BF16), (grad * up_term).astype(BF16)

    def back(gate_cot, up_cot, w_g, w_u):
        return (project_back(gate_cot, w_g) + project_back(up_cot, w_u)).astype(BF16)

    inners, inners_suf, pairs, sent, homes = {}, {}, {}, {}, {}

    def partial_of(d):
        pre = back(*inners[d][1:], w_pg, w_pu)
        suf = back(*inners_suf[d][1:], w_ag, w_au)
        return pre, suf

    def inner_of(d, *ties):
        cot, cot_suf = cot_chunks[d]
        terms, cot, *ties = after(inner_terms[d], cot, *ties)
        inners[d] = inner(terms[:3], cot, w_pd)
        inners_suf[d] = inner(terms[3:], cot_suf, w_ad)
        return ties

    order = list(range(1, dp)) + [0]
    inner_of(0)
    last = inners[0][0]
    for i, d in enumerate(order):
        if d > 0:
            inner_of(d, last)
        if i > 0:
            e = order[i - 1]
            *inners[d], pairs[e] = after(*inners[d], pairs[e])
            keep, got = pairs[e][0], pairs[e][1]
            keep, send = pack.second(keep, got)
            *inners[d], send = after(*inners[d], send)
            pairs[e] = keep, swap(send, "tp", 4, 2)
        pre, suf = partial_of(d)
        last = pre
        keep, send = pack.first(pre, suf)
        pairs[d] = keep, swap(send, "tp", 4, 1)
        if i > 1:
            e = order[i - 2]
            *pairs[d], keep, got = after(*pairs[d], *pairs[e])
            homes[e] = swap(pack.third(keep, got).astype(BF16), "dp", dp, e)
    def joined(values):
        return values if dp > 4 else [jnp.concatenate(values, axis=0)]

    def outer_chunks(left, right):
        return sum(outer_sum(a, b) for a, b in zip(joined(left), joined(right)))

    def columns_back(i):
        pre = outer_chunks([n[0] for n in normed_late], [inners[d][i] for d in range(dp)])
        act = outer_chunks([n[1] for n in normed_late], [inners_suf[d][i] for d in range(dp)])
        pre = pre.astype(BF16).reshape(shards, d_slice, hid)
        act = halves_down(act.astype(BF16).reshape(shards, a_slice, hid_act), 2)
        whole = jnp.concatenate([pre, act], axis=2).reshape(dp, 2, d_slice, -1)
        return whole[:, 0], whole[:, 1]

    def both_sum(own, got):
        return (own.astype(F32) + got.astype(F32)).astype(BF16)

    def columns_end(whole):
        pre = jnp.concatenate([whole[i, :, :hid] for i in range(dp)], axis=1)
        act = halves_down(whole[:, :, hid:], 1)
        act = jnp.concatenate([act[i] for i in range(dp)], axis=1)
        return pre.astype(F32), act.astype(F32)

    hiddens = [inners[d][0] for d in range(dp)]
    hid_suf = [inners_suf[d][0] for d in range(dp)]
    last, normed_late, cot_late, pairs[0] = after(last, normed_chunks, cot_chunks, pairs[0])
    keep, send = pack.second(*pairs[0])
    pairs[0] = keep, swap(send, "tp", 4, 2)
    normed_late, send = after(normed_late, send)
    gate_own, gate_send = columns_back(1)
    gate_got = swap(gate_send, "expert", 2, 1)
    for e in order[-2:-1]:
        gate_send, keep, got = after(gate_send, *pairs[e])
        homes[e] = swap(pack.third(keep, got).astype(BF16), "dp", dp, e)
    hiddens, gate_send = after(hiddens, gate_send)
    outs = jnp.concatenate([project(h, w_pd).astype(BF16) for h in hiddens], axis=0)
    outs_suf = project(jnp.concatenate(hid_suf, axis=0), w_ad).astype(BF16)
    outs_keep, outs_send = pack.first(outs, outs_suf)
    outs_got = swap(outs_send, "tp", 4, 1)
    outs_got, keep, got, normed_late = after(outs_got, *pairs[0], normed_late)
    home = pack.third(keep, got)
    outs_keep, outs_send = pack.second(outs_keep, outs_got)
    outs_got = swap(outs_send, "tp", 4, 2)
    up_own, up_send = columns_back(2)

    for d in range(1, dp):
        home = home + homes[d].astype(F32)
    mcot, mcot_suf = undo_block(home)
    mid_part, ffn_gain = norm_back(resid, gain_pf, mcot)
    mid_part_suf, ffn_gain_suf = norm_back(resid_suf, gain_af, mcot_suf)
    mid = cot_mine.astype(F32) + mid_part
    mid_suf = cot_suf_mine.astype(F32) + mid_part_suf
    mid_block, hiddens = after(pack.join(mid, mid_suf).astype(BF16), hiddens)
    bcot, bcot_suf = pack.tp_gather(mid_block)
    down_pre = outer_chunks(hiddens, [c[0] for c in cot_late]).astype(BF16)
    down_act = outer_chunks(hid_suf, [c[1] for c in cot_late]).astype(BF16)
    pre_blocks, act_blocks = column_blocks(down_pre, shards), column_blocks(down_act, shards)

    def down_half(i):
        act = halves_down(jnp.stack(act_blocks[i::2]), 1)
        return jnp.concatenate([jnp.stack(pre_blocks[i::2]), act], axis=1)

    down_own, down_send = down_half(0), down_half(1)
    bcot, bcot_suf, gate_got, up_send = after(bcot, bcot_suf, gate_got, up_send)
    gate_grad = dp_move(both_sum(gate_own, gate_got))
    up_got = swap(up_send, "expert", 2, 1)
    bcot, outs_got = after(bcot, outs_got)
    outs = pack.third(outs_keep, outs_got)
    outs = [outs[:1]] + [
        swap(outs[d : d + 1].astype(BF16), "dp", dp, d).astype(F32) for d in range(1, dp)
    ]
    acot_pre = project_back(bcot, w_po).astype(BF16)
    acot_suf = project_back(bcot_suf, w_ao).astype(BF16)
    qcot_pre, qcot_suf, kcot, vcot = attend_back(
        info, queries_pre, queries_suf, keys, values, acot_pre, acot_suf, pre_items, suf_len
    )
    got = swap(jnp.where(core == 0, vcot, kcot).astype(BF16), "tp", 4, 1)
    kvcot = jnp.where(core == 0, kcot, vcot) + got.astype(F32)
    kv_pre_cot = kvcot[: pre_items * full_len].reshape(pre_items, 2, half_rows, HD)
    got = swap(kv_pre_cot[:, 1].astype(BF16), "expert", 2, 1)
    kv_pre_cot = kv_pre_cot[:, 0] + got.astype(F32)
    kvcot = jnp.concatenate(
        [kv_pre_cot.reshape(rows, HD), kvcot[pre_items * full_len :]], axis=0
    )
    kvcot, att_pre, att_suf = after(kvcot, att_pre, att_suf)
    got = swap(kvcot.astype(BF16), "tp", 4, 2)
    kvcot = (kvcot + got.astype(F32)).astype(BF16)
    kvcot, gate_grad, up_got, down_send = after(kvcot, gate_grad, up_got, down_send)
    up_grad = dp_move(both_sum(up_own, up_got))
    down_got = swap(down_send, "expert", 2, 1)
    key_half, key_own = kvcot[:rows], kvcot[rows:]
    ncot = project_back(qcot_pre, w_pq) + 0.5 * project_back(key_half, w_pkv)
    ncot_suf = project_back(qcot_suf, w_aq) + 0.5 * project_back(key_own, w_akv)
    ncot, ncot_suf = pack.tp_sum(ncot, ncot_suf)
    in_part, attn_gain = norm_back(x_mine, gain_pa, ncot)
    in_part_suf, attn_gain_suf = norm_back(xs_mine, gain_aa, ncot_suf)
    grad_mine = mid + in_part
    grad_suf_mine = mid_suf + in_part_suf
    embed_w = lax.dot_general(
        own_suffix(chosen).astype(F32),
        grad_suf_mine,
        (((0,), (0,)), ((), ())),
        precision=lax.Precision.HIGHEST,
    )
    tail = jnp.concatenate(
        [
            attn_gain.reshape(shards, -1),
            ffn_gain.reshape(shards, -1),
            attn_gain_suf.reshape(shards, -1),
            ffn_gain_suf.reshape(shards, -1),
            embed_w.reshape(shards, -1),
        ],
        axis=1,
    )

    out_w = jnp.concatenate(
        [
            jnp.stack(column_blocks(outer_sum(att_pre, bcot).astype(BF16), shards)),
            jnp.stack(column_blocks(outer_sum(att_suf, bcot_suf).astype(BF16), shards)),
        ],
        axis=2,
    )
    in_w = jnp.concatenate(
        [
            jnp.concatenate(
                [
                    outer_sum(normed_pre, qcot_pre).astype(BF16).reshape(shards, d_slice, q_cols),
                    outer_sum(normed_pre, key_half).astype(BF16).reshape(shards, d_slice, HD),
                ],
                axis=2,
            ),
            jnp.concatenate(
                [
                    outer_sum(normed_suf, qcot_suf).astype(BF16).reshape(shards, a_slice, q_cols),
                    outer_sum(normed_suf, key_own).astype(BF16).reshape(shards, a_slice, HD),
                ],
                axis=2,
            ),
        ],
        axis=1,
    )

    def scatter_y(value):
        value = value.reshape((dp, 2) + value.shape[1:])
        send = lax.dynamic_index_in_dim(value, 1 - group, 1, keepdims=False)
        keep = lax.dynamic_index_in_dim(value, group, 1, keepdims=False)
        return keep, swap(send, "expert", 2, 1)

    def scatter_z(moved):
        return jnp.sum(dp_move(both_sum(*moved)).astype(F32), axis=0)

    out_w = scatter_y(out_w)
    in_w = scatter_y(in_w)
    in_w, up_grad, down_got = after(in_w, up_grad, down_got)
    down_grad = dp_move(both_sum(down_own, down_got))
    tail = tail + swap(tail, "tp", 4, 1)
    tail = tail + swap(tail, "tp", 4, 2)
    tail_own, tail_got = scatter_y(tail)
    tail_size = tail.shape[1]
    tail_rows = -(-tail_size // (16 * w1)) * 16
    tail = jnp.pad(tail_own + tail_got, ((0, 0), (0, tail_rows * w1 - tail_size)))
    out_w = scatter_z(out_w)
    in_w = both_sum(*in_w)
    in_rows = in_w.shape[1]
    in_w = jnp.concatenate([in_w, tail.reshape(dp, tail_rows, w1).astype(BF16)], axis=1)
    in_w = jnp.sum(dp_move(in_w).astype(F32), axis=0)
    tail = in_w[in_rows:].reshape(-1)[:tail_size]
    in_w = in_w[:in_rows]
    g_po, g_ao = out_w[:, :d_slice], out_w[:, d_slice:]
    g_pq, g_aq = in_w[:d_slice, :q_cols], in_w[d_slice:, :q_cols]
    kv_w = in_w[:, q_cols:].astype(BF16)
    kv_other = swap(kv_w, "tp", 4, 1).astype(F32)
    kv_w = kv_w.astype(F32)
    kv_w = jnp.concatenate(
        [jnp.where(core == 0, kv_w, kv_other), jnp.where(core == 0, kv_other, kv_w)], axis=1
    )
    g_pkv, g_akv = kv_w[:d_slice], kv_w[d_slice:]

    out_pre, out_suf = undo_block(sum(outs))
    out_block = pack.join(resid + out_pre, resid_suf + out_suf).astype(BF16)
    out_pre, out_suf = pack.tp_gather(out_block)
    prefix_out = out_pre.reshape(pre_items, half_rows, width)
    suffix_out = out_suf[None, :suf_len]
    grad_pre, grad_suf = pack.tp_gather(pack.join(grad_mine, grad_suf_mine).astype(BF16))
    prefix_grad = grad_pre.astype(F32).reshape(pre_items, half_rows, width)
    suffix_grad = grad_suf.astype(F32)[None, :suf_len]
    g_pg, g_ag = columns_end(gate_grad)
    g_pu, g_au = columns_end(up_grad)
    g_pd = down_grad[:, :hid].reshape(dp * hid, d_slice).astype(F32)
    g_ad = halves_down(down_grad[:, hid:], 2).reshape(dp * hid_act, a_slice).astype(F32)
    tails, at = [], 0
    for size in (d_slice, d_slice, a_slice, a_slice, action_embed.size):
        tails.append(tail[at : at + size])
        at += size
    g_gpa, g_gpf, g_gaa, g_gaf, g_embed = tails
    g_embed = g_embed.reshape(action_embed.shape)
    return (
        prefix_out,
        suffix_out,
        prefix_grad,
        suffix_grad,
        g_pq,
        g_pkv,
        g_po,
        g_pg,
        g_pu,
        g_pd,
        g_gpa,
        g_gpf,
        g_aq,
        g_akv,
        g_ao,
        g_ag,
        g_au,
        g_ad,
        g_gaa,
        g_gaf,
        g_embed,
    )


def solution(mesh):
    return jax.shard_map(
        functools.partial(local, mesh.shape["dp"]),
        mesh=mesh,
        in_specs=(
            P("dp", "expert", None),
            P(("dp", "expert"), None, None),
            P(("dp", "expert"), None, None),
            P("dp"),
            P(("dp", "expert"), None),
            P(("dp", "expert"), "tp"),
            P(("dp", "expert"), None),
            P("tp", ("dp", "expert")),
            P(("dp", "expert"), "tp"),
            P(("dp", "expert"), "tp"),
            P("tp", ("dp", "expert")),
            P(("dp", "expert")),
            P(("dp", "expert")),
            P(("dp", "expert"), "tp"),
            P(("dp", "expert"), None),
            P("tp", ("dp", "expert")),
            P(("dp", "expert"), "tp"),
            P(("dp", "expert"), "tp"),
            P("tp", ("dp", "expert")),
            P(("dp", "expert")),
            P(("dp", "expert")),
            P(("dp", "expert"), None),
            P("dp", "expert", None),
            P(("dp", "expert"), None, None),
        ),
        out_specs=(
            P("dp", "expert", None),
            P(("dp", "expert"), None, None),
            P("dp", "expert", None),
            P(("dp", "expert"), None, None),
            P(("dp", "expert"), "tp"),
            P(("dp", "expert"), None),
            P("tp", ("dp", "expert")),
            P(("dp", "expert"), "tp"),
            P(("dp", "expert"), "tp"),
            P("tp", ("dp", "expert")),
            P(("dp", "expert")),
            P(("dp", "expert")),
            P(("dp", "expert"), "tp"),
            P(("dp", "expert"), None),
            P("tp", ("dp", "expert")),
            P(("dp", "expert"), "tp"),
            P(("dp", "expert"), "tp"),
            P("tp", ("dp", "expert")),
            P(("dp", "expert")),
            P(("dp", "expert")),
            P(("dp", "expert"), None),
        ),
        check_vma=False,
    )
```

```python
import functools

import jax
import jax.numpy as jnp
from jax import lax
from jax.experimental import pallas as pl
from jax.experimental.pallas import tpu as pltpu
from jax.sharding import PartitionSpec as P

HD = 256
EPSILON = 1e-06
PAD = 64
F32 = jnp.float32
BF16 = jnp.bfloat16


def rms_scale(values, gain):
    return values * lax.rsqrt(jnp.mean(values * values, axis=-1, keepdims=True) + EPSILON) * gain


def gelu_tanh(values):
    return jax.nn.gelu(values, approximate=True)


def geglu(gate, upward):
    return gelu_tanh(gate) * upward


def project(left, right):
    return jnp.dot(left, right, preferred_element_type=F32)


def project_back(left, right):
    return lax.dot_general(left, right, (((1,), (1,)), ((), ())), preferred_element_type=F32)


def outer_sum(left, right):
    return lax.dot_general(left, right, (((0,), (0,)), ((), ())), preferred_element_type=F32)


def norm_back(values, gain, cotangent):
    return jax.vjp(rms_scale, values, gain.astype(F32))[1](cotangent)


MIB = 1024 * 1024


def key_mask(shape, start, length, group, half_rows):
    place = lax.broadcasted_iota(jnp.int32, shape, 1)
    own = jnp.where(place < half_rows, group, 1 - group) * half_rows
    place = jnp.where(place < half_rows, place, place - half_rows) + own
    return place < length


def softmax_parts(scores):
    top = functools.reduce(jnp.maximum, [jnp.max(s, axis=1, keepdims=True) for s in scores])
    expo = [jnp.exp(s - top) for s in scores]
    denom = sum(jnp.sum(e, axis=1, keepdims=True) for e in expo)
    return [e / denom for e in expo]


def suffix_scores(q, keys, own_keys, live, later, scale):
    first = jnp.where(live, project_back(q, keys) * scale, -1e30)
    second = jnp.where(later, project_back(q, own_keys) * scale, -1e30)
    return softmax_parts([first, second])


def suffix_masks(suf_len, full, length, group, half_rows):
    live = key_mask((PAD, full), 0, length, group, half_rows)
    row = lax.broadcasted_iota(jnp.int32, (PAD, PAD), 0)
    column = lax.broadcasted_iota(jnp.int32, (PAD, PAD), 1)
    later = ((column == 0) | (row > 0)) & (column < suf_len)
    return live, later


def attend_kernel(items, heads, suf_len, info, q, qs, k, v, att, att_suf):
    scale = HD ** (-0.5)
    rows = q.shape[0] // items
    full = (k.shape[0] - PAD) // items
    group = info[0]
    for i in range(items):
        live = key_mask((rows, full), 0, info[1 + i], group, rows)
        for h in range(heads):
            at, keys = (slice(i * rows, (i + 1) * rows), slice(h * HD, (h + 1) * HD)), slice(i * full, (i + 1) * full)
            scores = jnp.where(live, project_back(q[at], k[keys]) * scale, -1e30)
            (probs,) = softmax_parts([scores])
            att[at] = project(probs.astype(BF16), v[keys]).astype(BF16)
    live, later = suffix_masks(suf_len, full, info[1 + items], group, rows)
    start = pl.multiple_of(group * full, full)
    keys, values = k[pl.ds(start, full)], v[pl.ds(start, full)]
    own_keys, own_values = k[items * full :], v[items * full :]
    for h in range(heads):
        at = (slice(None), slice(h * HD, (h + 1) * HD))
        first, second = suffix_scores(qs[at], keys, own_keys, live, later, scale)
        total = project(first.astype(BF16), values) + project(second.astype(BF16), own_values)
        att_suf[at] = total.astype(BF16)


def attend_back_kernel(items, heads, suf_len, info, q, qs, k, v, cot, cot_suf, qcot, qcot_suf, kcot, vcot):
    scale = HD ** (-0.5)
    rows = q.shape[0] // items
    full = (k.shape[0] - PAD) // items
    group = info[0]
    for i in range(items):
        live = key_mask((rows, full), 0, info[1 + i], group, rows)
        for h in range(heads):
            at, keys = (slice(i * rows, (i + 1) * rows), slice(h * HD, (h + 1) * HD)), slice(i * full, (i + 1) * full)
            scores = jnp.where(live, project_back(q[at], k[keys]) * scale, -1e30)
            (probs,) = softmax_parts([scores])
            grad = project_back(cot[at], v[keys])
            delta = jnp.sum(probs * grad, axis=1, keepdims=True)
            inner = (probs * (grad - delta)).astype(BF16)
            qcot[at] = (project(inner, k[keys]) * scale).astype(BF16)
            kterm = outer_sum(inner, q[at]) * scale
            vterm = outer_sum(probs.astype(BF16), cot[at])
            if h == 0:
                kcot[keys], vcot[keys] = kterm, vterm
            else:
                kcot[keys] += kterm
                vcot[keys] += vterm
    live, later = suffix_masks(suf_len, full, info[1 + items], group, rows)
    start = pl.multiple_of(group * full, full)
    own = slice(items * full, items * full + PAD)
    place = pl.ds(start, full)
    for h in range(heads):
        at = (slice(None), slice(h * HD, (h + 1) * HD))
        first, second = suffix_scores(qs[at], k[place], k[own], live, later, scale)
        grads = project_back(cot_suf[at], v[place]), project_back(cot_suf[at], v[own])
        delta = sum(jnp.sum(p * g, axis=1, keepdims=True) for p, g in zip((first, second), grads))
        inners = [(p * (g - delta)).astype(BF16) for p, g in zip((first, second), grads)]
        total = project(inners[0], k[place]) + project(inners[1], k[own])
        qcot_suf[at] = (total * scale).astype(BF16)
        kcot[place] += outer_sum(inners[0], qs[at]) * scale
        vcot[place] += outer_sum(first.astype(BF16), cot_suf[at])
        kterm = outer_sum(inners[1], qs[at]) * scale
        vterm = outer_sum(second.astype(BF16), cot_suf[at])
        if h == 0:
            kcot[own], vcot[own] = kterm, vterm
        else:
            kcot[own] += kterm
            vcot[own] += vterm


def attention_call(kernel, name, out_shape, items, heads, suf_len, info, *arrays):
    spec = pl.BlockSpec(memory_space=pltpu.VMEM)
    return pl.pallas_call(
        functools.partial(kernel, items, heads, suf_len),
        in_specs=[pl.BlockSpec(memory_space=pltpu.SMEM)] + [spec] * len(arrays),
        out_specs=[spec] * len(out_shape),
        out_shape=out_shape,
        compiler_params=pltpu.CompilerParams(vmem_limit_bytes=32 * MIB),
        name=name,
    )(info, *arrays)


def attend(info, q, qs, k, v, items, suf_len):
    shape = [jax.ShapeDtypeStruct(q.shape, BF16), jax.ShapeDtypeStruct(qs.shape, BF16)]
    heads = q.shape[1] // HD
    return attention_call(attend_kernel, "attend", shape, items, heads, suf_len, info, q, qs, k, v)


def attend_back(info, q, qs, k, v, cot, cot_suf, items, suf_len):
    shape = [jax.ShapeDtypeStruct(a.shape, t) for a, t in ((q, BF16), (qs, BF16), (k, F32), (v, F32))]
    heads = q.shape[1] // HD
    return attention_call(
        attend_back_kernel, "attend_back", shape, items, heads, suf_len, info, q, qs, k, v, cot, cot_suf
    )


def swap(value, axis, size, mask):
    return lax.ppermute(value, axis, [(i, i ^ mask) for i in range(size)])


def column_blocks(value, count):
    width = value.shape[1] // count
    return [value[:, i * width : (i + 1) * width] for i in range(count)]


def halves_down(value, axis):
    other = value.ndim - 1 if axis == value.ndim - 2 else value.ndim - 2
    size = value.shape[axis] // 2
    first = lax.slice_in_dim(value, 0, size, axis=axis)
    second = lax.slice_in_dim(value, size, 2 * size, axis=axis)
    return jnp.concatenate([first, second], axis=other)


def after(*values):
    return lax.optimization_barrier(values)


def own_first(value, dp, group):
    width = value.shape[1] // (2 * dp)
    zero = jnp.zeros((), value.dtype)
    right = lax.pad(value, zero, ((0, 0, 0), (-width, width, 0)))
    left = lax.pad(value, zero, ((0, 0, 0), (width, -width, 0)))
    block = lax.broadcasted_iota(jnp.int32, value.shape, 1) // width
    return jnp.where(group == 0, value, jnp.where(block % 2 == 0, right, left))


class Rows:
    def __init__(self, part, suf_part, width, act_width, core, x_index):
        self.part, self.suf_part, self.core, self.x_index = part, suf_part, core, x_index
        self.width, self.act_width = width, act_width

    def join(self, pre, suf):
        zero = jnp.zeros((), suf.dtype)
        suf = lax.pad(suf, zero, ((0, 0, 0), (0, self.width - self.act_width, 0)))
        pre = pre.reshape(-1, self.part, self.width)
        return jnp.concatenate([pre, suf.reshape(-1, self.suf_part, self.width)], axis=1)

    def split(self, blocks):
        pre = blocks[:, : self.part].reshape(-1, self.width)
        return pre, blocks[:, self.part :, : self.act_width].reshape(-1, self.act_width)

    def tp_sum(self, pre, suf):
        whole = self.join(pre.astype(BF16), suf.astype(BF16))
        whole = whole.reshape(2, 2, -1, self.width)

        def pick(value, index, axis):
            return lax.dynamic_index_in_dim(value, index, axis, keepdims=False)

        got = swap(pick(whole, 1 - self.core, 1), "tp", 4, 1)
        pair = pick(whole, self.core, 1).astype(F32) + got.astype(F32)
        got = swap(pick(pair, 1 - self.x_index, 0).astype(BF16), "tp", 4, 2)
        return self.split((pick(pair, self.x_index, 0) + got.astype(F32))[None])

    def tp_gather(self, block):
        other = swap(block, "tp", 4, 2)
        low = jnp.where(self.x_index == 0, block, other)
        high = jnp.where(self.x_index == 0, other, block)
        pair = jnp.concatenate([low, high], axis=0)
        got = swap(pair, "tp", 4, 1)
        even = jnp.where(self.core == 0, pair, got)
        odd = jnp.where(self.core == 0, got, pair)
        return self.split(jnp.stack([even, odd], axis=1).reshape(4, -1, self.width))

    def spread(self, block, far):
        pair = jnp.concatenate([block, far], axis=0)
        return self.split(jnp.concatenate([pair, swap(pair, "tp", 4, 1)], axis=0))

    def first(self, pre, suf):
        whole = self.join(pre, suf).reshape(-1, 4, self.part + self.suf_part, self.width)
        return whole[:, :2], whole[:, 2:]

    def second(self, keep, got):
        pair = keep.astype(F32) + got.astype(F32)
        return pair[:, 0], pair[:, 1].astype(BF16)

    def third(self, keep, got):
        return keep + got.astype(F32)


def local(
    dp,
    prefix_in,
    suffix_in,
    noisy_actions,
    prefix_len,
    action_live,
    pre_query,
    pre_keyval,
    pre_output,
    pre_gate,
    pre_up,
    pre_down,
    pre_norm_attn,
    pre_norm_ffn,
    act_query,
    act_keyval,
    act_output,
    act_gate,
    act_up,
    act_down,
    act_norm_attn,
    act_norm_ffn,
    action_embed,
    prefix_cot,
    suffix_cot,
):
    shards = 2 * dp
    both = ("dp", "expert")
    group = lax.axis_index("expert")
    t_index = lax.axis_index("tp")
    core, x_index = lax.rem(t_index, 2), t_index // 2
    pre_items, half_rows, width = prefix_in.shape
    _, suf_len, act_width = suffix_in.shape
    rows = pre_items * half_rows
    part = rows // 4
    suf_part = PAD // 4
    pack = Rows(part, suf_part, width, act_width, core, x_index)
    d_slice, q_cols = pre_query.shape
    a_slice = act_query.shape[0]
    hid = pre_gate.shape[1] // dp
    hid_act = act_gate.shape[1] // dp

    def half_cols(value):
        return lax.dynamic_slice_in_dim(value, core * HD, HD, 1)

    w1 = q_cols + HD
    small = [pre_norm_attn, pre_norm_ffn, act_norm_attn, act_norm_ffn, action_embed.reshape(-1)]
    small = jnp.concatenate(small)
    small_rows = -(-small.shape[0] // (16 * w1)) * 16
    small = jnp.pad(small, (0, small_rows * w1 - small.shape[0])).reshape(small_rows, w1)
    packed_in = jnp.concatenate(
        [
            jnp.concatenate([pre_query, half_cols(pre_keyval)], axis=1),
            jnp.concatenate([act_query, half_cols(act_keyval)], axis=1),
            small,
        ],
        axis=0,
    )
    z_index = lax.axis_index("dp")
    in_z = [packed_in] + [swap(packed_in, "dp", dp, d) for d in range(1, dp)]
    in_far = [swap(packed_in, "expert", 2, 1)]

    def columns_out(pre, act):
        act_blocks = halves_down(jnp.stack(column_blocks(act, dp)), 2)
        return jnp.concatenate([jnp.stack(column_blocks(pre, dp)), act_blocks], axis=2)

    def columns_in(moved, pre, act):
        halves = jnp.stack(moved, axis=1)
        w_pre = halves[..., :hid].reshape(width, hid)
        w_act = halves_down(halves[..., hid:], 2).reshape(act_width, hid_act)
        return w_pre, w_act

    def dp_move(value):
        return lax.all_to_all(value, "dp", 0, 0, tiled=True)

    gate_out = columns_out(pre_gate, act_gate)
    up_out = columns_out(pre_up, act_up)
    down_out = jnp.concatenate(
        [
            pre_down.reshape(dp, hid, d_slice),
            halves_down(act_down.reshape(dp, hid_act, a_slice), 1),
        ],
        axis=1,
    )
    packed_out = jnp.concatenate([pre_output, act_output], axis=1)

    def own_rows(value):
        return lax.dynamic_slice_in_dim(value, t_index * part, part, 0)

    def own_suffix(value):
        return lax.dynamic_slice_in_dim(value, t_index * suf_part, suf_part, 0)

    def pad_suffix(value):
        return jnp.pad(value, ((0, PAD - suf_len), (0, 0)))

    def own_block(pre, suf):
        return pack.join(own_first(pre, dp, group), own_first(suf, dp, group))

    def undo_block(block):
        pre, suf = pack.split(block)
        return own_first(pre, dp, group), own_first(suf, dp, group)

    cot_mine = own_rows(prefix_cot.reshape(rows, width))
    cot_suf_mine = own_suffix(pad_suffix(suffix_cot[0]))
    cot_block = own_block(cot_mine, cot_suf_mine)

    gate_own = dp_move(gate_out)
    full_out = lax.all_gather(packed_out, both, axis=0)
    *in_z, gate_own, up_out = after(*in_z, gate_own, up_out)
    in_far += [swap(block, "expert", 2, 1) for block in in_z[1:]]
    up_own = dp_move(up_out)
    full_in = jnp.zeros((dp, 2) + packed_in.shape, BF16)
    for d in range(dp):
        z = jnp.bitwise_xor(z_index, d)
        full_in = lax.dynamic_update_slice(full_in, in_z[d][None, None], (z, group, 0, 0))
        full_in = lax.dynamic_update_slice(full_in, in_far[d][None, None], (z, 1 - group, 0, 0))
    full_in = full_in.reshape((shards,) + packed_in.shape)

    w_pq = full_in[:, :d_slice, :q_cols].reshape(width, q_cols)
    w_pkv = full_in[:, :d_slice, q_cols:].reshape(width, HD)
    w_aq = full_in[:, d_slice : d_slice + a_slice, :q_cols].reshape(act_width, q_cols)
    w_akv = full_in[:, d_slice : d_slice + a_slice, q_cols:].reshape(act_width, HD)
    rest = full_in[:, d_slice + a_slice :].reshape(shards, small_rows * w1)
    gains, at = [], 0
    for size in (d_slice, d_slice, a_slice, a_slice):
        gains.append(rest[:, at : at + size].reshape(1, shards * size).astype(F32))
        at += size
    gain_pa, gain_pf, gain_aa, gain_af = gains
    embed = rest[:, at : at + action_embed.size].reshape(-1, act_width)
    prefix_x = prefix_in.astype(F32).reshape(rows, width)
    chosen = jnp.where(
        action_live[0][None, :] == 1, noisy_actions[0], jnp.zeros_like(noisy_actions[0])
    )
    chosen = jnp.pad(chosen, ((1, PAD - suf_len), (0, 0)))
    suffix_x = pad_suffix(suffix_in[0].astype(F32)) + project(chosen, embed)
    normed_pre = rms_scale(prefix_x, gain_pa).astype(BF16)
    normed_suf = rms_scale(suffix_x, gain_aa).astype(BF16)
    kv_pre = project(normed_pre, w_pkv).astype(BF16)
    kv_pre = kv_pre.reshape(pre_items, half_rows, HD)
    kv_got = swap(kv_pre, "expert", 2, 1)
    kv_suf = project(normed_suf, w_akv).astype(BF16)
    queries_pre = project(normed_pre, w_pq).astype(BF16)
    queries_suf = project(normed_suf, w_aq).astype(BF16)
    queries_pre, queries_suf, kv_suf, kv_got, gate_own, up_own, down_out = after(
        queries_pre, queries_suf, kv_suf, kv_got, gate_own, up_own, down_out
    )
    down_own = dp_move(down_out)
    gate_got = swap(gate_own, "expert", 2, 1)
    kv_pre = jnp.concatenate([kv_pre, kv_got], axis=1)
    full_len = kv_pre.shape[1]
    kv_mine = jnp.concatenate([kv_pre.reshape(pre_items * full_len, HD), kv_suf], axis=0)
    kv_other = swap(kv_mine, "tp", 4, 1)
    keys = jnp.where(core == 0, kv_mine, kv_other)
    values = jnp.where(core == 0, kv_other, kv_mine)

    own_len = lax.dynamic_slice_in_dim(prefix_len, group, 1)
    info = jnp.concatenate([group.reshape(1).astype(jnp.int32), prefix_len, own_len])
    att_pre, att_suf = attend(info, queries_pre, queries_suf, keys, values, pre_items, suf_len)
    att_pre, att_suf, full_out = after(att_pre, att_suf, full_out)
    w_po = jnp.concatenate([full_out[i, :, :d_slice] for i in range(shards)], axis=1)
    w_ao = jnp.concatenate([full_out[i, :, d_slice:] for i in range(shards)], axis=1)
    x_mine = own_rows(prefix_in.reshape(rows, width)).astype(F32)
    xs_mine = own_suffix(suffix_x)
    branch = pack.tp_sum(project(att_pre, w_po), project(att_suf, w_ao))
    branch, branch_suf = branch
    resid = x_mine + branch
    resid_suf = xs_mine + branch_suf
    normed_block = own_block(
        rms_scale(resid, gain_pf).astype(BF16), rms_scale(resid_suf, gain_af).astype(BF16)
    )

    normed_far = swap(normed_block, "tp", 4, 2)
    normed_z = [normed_block] + [swap(normed_block, "dp", dp, d) for d in range(1, dp)]
    normed_far, up_own, gate_got = after(normed_far, up_own, gate_got)
    up_got = swap(up_own, "expert", 2, 1)
    normed_z[-1], down_own = after(normed_z[-1], down_own)
    w_pg, w_ag = columns_in((gate_own, gate_got), pre_gate, act_gate)
    normed_chunks, gates, inner_terms = [], [], []

    def gelu_terms(gate):
        value, pull = jax.vjp(gelu_tanh, gate)
        return value, pull(jnp.ones_like(gate))[0]

    def scale_terms(gate, upward):
        value, slope = gate
        return (value * upward).astype(BF16), upward * slope, value

    for d in range(dp):
        far = normed_far if d == 0 else swap(normed_z[d], "tp", 4, 2)
        pre, suf = pack.spread(normed_z[d], far)
        if d > 0:
            pre, suf, *gates[-1] = after(pre, suf, *gates[-1])
        normed_chunks.append((pre, suf))
        gates.append((gelu_terms(project(pre, w_pg)), gelu_terms(project(suf, w_ag))))
    gates[0], cot_block = after(gates[0], cot_block)
    cot_z = [swap(cot_block, "dp", dp, d) for d in range(1, dp)]
    gates[-1], up_got, down_own = after(gates[-1], up_got, down_own)
    down_got = swap(down_own, "expert", 2, 1)
    w_pu, w_au = columns_in((up_own, up_got), pre_up, act_up)
    for d in range(dp):
        pre, suf = normed_chunks[d]
        terms = scale_terms(gates[d][0], project(pre, w_pu))
        terms += scale_terms(gates[d][1], project(suf, w_au))
        inner_terms.append(after(*terms))
    cot_far = swap(cot_block, "tp", 4, 2)
    inner_terms[0], cot_far = after(inner_terms[0], cot_far)
    cot_chunks = [pack.spread(cot_block, cot_far)]
    cot_chunks += [pack.spread(z, swap(z, "tp", 4, 2)) for z in cot_z]
    down = jnp.stack([down_own, down_got], axis=1).reshape(shards, hid + hid_act // 2, d_slice)
    w_pd = jnp.concatenate([down[i, :hid] for i in range(shards)], axis=1)
    act_down_blocks = halves_down(down[:, hid:], 2)
    w_ad = jnp.concatenate([act_down_blocks[i] for i in range(shards)], axis=1)

    def inner(terms, cot, w_d):
        hidden, gate_term, up_term = terms
        grad = project_back(cot, w_d)
        return hidden, (grad * gate_term).astype(BF16), (grad * up_term).astype(BF16)

    def back(gate_cot, up_cot, w_g, w_u):
        return (project_back(gate_cot, w_g) + project_back(up_cot, w_u)).astype(BF16)

    inners, inners_suf, pairs, sent, homes = {}, {}, {}, {}, {}

    def partial_of(d):
        pre = back(*inners[d][1:], w_pg, w_pu)
        suf = back(*inners_suf[d][1:], w_ag, w_au)
        return pre, suf

    def inner_of(d, *ties):
        cot, cot_suf = cot_chunks[d]
        terms, cot, *ties = after(inner_terms[d], cot, *ties)
        inners[d] = inner(terms[:3], cot, w_pd)
        inners_suf[d] = inner(terms[3:], cot_suf, w_ad)
        return ties

    order = list(range(1, dp)) + [0]
    inner_of(0)
    last = inners[0][0]
    for i, d in enumerate(order):
        if d > 0:
            inner_of(d, last)
        if i > 0:
            e = order[i - 1]
            *inners[d], pairs[e] = after(*inners[d], pairs[e])
            keep, got = pairs[e][0], pairs[e][1]
            keep, send = pack.second(keep, got)
            *inners[d], send = after(*inners[d], send)
            pairs[e] = keep, swap(send, "tp", 4, 2)
        pre, suf = partial_of(d)
        last = pre
        keep, send = pack.first(pre, suf)
        pairs[d] = keep, swap(send, "tp", 4, 1)
        if i > 1:
            e = order[i - 2]
            *pairs[d], keep, got = after(*pairs[d], *pairs[e])
            homes[e] = swap(pack.third(keep, got).astype(BF16), "dp", dp, e)
    def joined(values):
        return values if dp > 4 else [jnp.concatenate(values, axis=0)]

    def outer_chunks(left, right):
        return sum(outer_sum(a, b) for a, b in zip(joined(left), joined(right)))

    def columns_back(i):
        pre = outer_chunks([n[0] for n in normed_late], [inners[d][i] for d in range(dp)])
        act = outer_chunks([n[1] for n in normed_late], [inners_suf[d][i] for d in range(dp)])
        pre = pre.astype(BF16).reshape(shards, d_slice, hid)
        act = halves_down(act.astype(BF16).reshape(shards, a_slice, hid_act), 2)
        whole = jnp.concatenate([pre, act], axis=2).reshape(dp, 2, d_slice, -1)
        return whole[:, 0], whole[:, 1]

    def both_sum(own, got):
        return (own.astype(F32) + got.astype(F32)).astype(BF16)

    def columns_end(whole):
        pre = jnp.concatenate([whole[i, :, :hid] for i in range(dp)], axis=1)
        act = halves_down(whole[:, :, hid:], 1)
        act = jnp.concatenate([act[i] for i in range(dp)], axis=1)
        return pre.astype(F32), act.astype(F32)

    hiddens = [inners[d][0] for d in range(dp)]
    hid_suf = [inners_suf[d][0] for d in range(dp)]
    last, normed_late, cot_late, pairs[0] = after(last, normed_chunks, cot_chunks, pairs[0])
    keep, send = pack.second(*pairs[0])
    pairs[0] = keep, swap(send, "tp", 4, 2)
    normed_late, send = after(normed_late, send)
    gate_own, gate_send = columns_back(1)
    gate_got = swap(gate_send, "expert", 2, 1)
    for e in order[-2:-1]:
        gate_send, keep, got = after(gate_send, *pairs[e])
        homes[e] = swap(pack.third(keep, got).astype(BF16), "dp", dp, e)
    hiddens, gate_send = after(hiddens, gate_send)
    outs = jnp.concatenate([project(h, w_pd).astype(BF16) for h in hiddens], axis=0)
    outs_suf = project(jnp.concatenate(hid_suf, axis=0), w_ad).astype(BF16)
    outs_keep, outs_send = pack.first(outs, outs_suf)
    outs_got = swap(outs_send, "tp", 4, 1)
    outs_got, keep, got, normed_late = after(outs_got, *pairs[0], normed_late)
    home = pack.third(keep, got)
    outs_keep, outs_send = pack.second(outs_keep, outs_got)
    outs_got = swap(outs_send, "tp", 4, 2)
    up_own, up_send = columns_back(2)

    for d in range(1, dp):
        home = home + homes[d].astype(F32)
    mcot, mcot_suf = undo_block(home)
    mid_part, ffn_gain = norm_back(resid, gain_pf, mcot)
    mid_part_suf, ffn_gain_suf = norm_back(resid_suf, gain_af, mcot_suf)
    mid = cot_mine.astype(F32) + mid_part
    mid_suf = cot_suf_mine.astype(F32) + mid_part_suf
    mid_block, hiddens = after(pack.join(mid, mid_suf).astype(BF16), hiddens)
    bcot, bcot_suf = pack.tp_gather(mid_block)
    down_pre = outer_chunks(hiddens, [c[0] for c in cot_late]).astype(BF16)
    down_act = outer_chunks(hid_suf, [c[1] for c in cot_late]).astype(BF16)
    pre_blocks, act_blocks = column_blocks(down_pre, shards), column_blocks(down_act, shards)

    def down_half(i):
        act = halves_down(jnp.stack(act_blocks[i::2]), 1)
        return jnp.concatenate([jnp.stack(pre_blocks[i::2]), act], axis=1)

    down_own, down_send = down_half(0), down_half(1)
    bcot, bcot_suf, gate_got, up_send = after(bcot, bcot_suf, gate_got, up_send)
    gate_grad = dp_move(both_sum(gate_own, gate_got))
    up_got = swap(up_send, "expert", 2, 1)
    bcot, outs_got = after(bcot, outs_got)
    outs = pack.third(outs_keep, outs_got)
    outs = [outs[:1]] + [
        swap(outs[d : d + 1].astype(BF16), "dp", dp, d).astype(F32) for d in range(1, dp)
    ]
    acot_pre = project_back(bcot, w_po).astype(BF16)
    acot_suf = project_back(bcot_suf, w_ao).astype(BF16)
    qcot_pre, qcot_suf, kcot, vcot = attend_back(
        info, queries_pre, queries_suf, keys, values, acot_pre, acot_suf, pre_items, suf_len
    )
    got = swap(jnp.where(core == 0, vcot, kcot).astype(BF16), "tp", 4, 1)
    kvcot = jnp.where(core == 0, kcot, vcot) + got.astype(F32)
    kv_pre_cot = kvcot[: pre_items * full_len].reshape(pre_items, 2, half_rows, HD)
    got = swap(kv_pre_cot[:, 1].astype(BF16), "expert", 2, 1)
    kv_pre_cot = kv_pre_cot[:, 0] + got.astype(F32)
    kvcot = jnp.concatenate(
        [kv_pre_cot.reshape(rows, HD), kvcot[pre_items * full_len :]], axis=0
    )
    kvcot, att_pre, att_suf = after(kvcot, att_pre, att_suf)
    got = swap(kvcot.astype(BF16), "tp", 4, 2)
    kvcot = (kvcot + got.astype(F32)).astype(BF16)
    kvcot, gate_grad, up_got, down_send = after(kvcot, gate_grad, up_got, down_send)
    up_grad = dp_move(both_sum(up_own, up_got))
    down_got = swap(down_send, "expert", 2, 1)
    key_half, key_own = kvcot[:rows], kvcot[rows:]
    ncot = project_back(qcot_pre, w_pq) + 0.5 * project_back(key_half, w_pkv)
    ncot_suf = project_back(qcot_suf, w_aq) + 0.5 * project_back(key_own, w_akv)
    ncot, ncot_suf = pack.tp_sum(ncot, ncot_suf)
    in_part, attn_gain = norm_back(x_mine, gain_pa, ncot)
    in_part_suf, attn_gain_suf = norm_back(xs_mine, gain_aa, ncot_suf)
    grad_mine = mid + in_part
    grad_suf_mine = mid_suf + in_part_suf
    embed_w = lax.dot_general(
        own_suffix(chosen).astype(F32),
        grad_suf_mine,
        (((0,), (0,)), ((), ())),
        precision=lax.Precision.HIGHEST,
    )
    tail = jnp.concatenate(
        [
            attn_gain.reshape(shards, -1),
            ffn_gain.reshape(shards, -1),
            attn_gain_suf.reshape(shards, -1),
            ffn_gain_suf.reshape(shards, -1),
            embed_w.reshape(shards, -1),
        ],
        axis=1,
    )

    out_w = jnp.concatenate(
        [
            jnp.stack(column_blocks(outer_sum(att_pre, bcot).astype(BF16), shards)),
            jnp.stack(column_blocks(outer_sum(att_suf, bcot_suf).astype(BF16), shards)),
        ],
        axis=2,
    )
    in_w = jnp.concatenate(
        [
            jnp.concatenate(
                [
                    outer_sum(normed_pre, qcot_pre).astype(BF16).reshape(shards, d_slice, q_cols),
                    outer_sum(normed_pre, key_half).astype(BF16).reshape(shards, d_slice, HD),
                ],
                axis=2,
            ),
            jnp.concatenate(
                [
                    outer_sum(normed_suf, qcot_suf).astype(BF16).reshape(shards, a_slice, q_cols),
                    outer_sum(normed_suf, key_own).astype(BF16).reshape(shards, a_slice, HD),
                ],
                axis=2,
            ),
        ],
        axis=1,
    )

    def scatter_y(value):
        value = value.reshape((dp, 2) + value.shape[1:])
        send = lax.dynamic_index_in_dim(value, 1 - group, 1, keepdims=False)
        keep = lax.dynamic_index_in_dim(value, group, 1, keepdims=False)
        return keep, swap(send, "expert", 2, 1)

    def scatter_z(moved):
        return jnp.sum(dp_move(both_sum(*moved)).astype(F32), axis=0)

    out_w = scatter_y(out_w)
    in_w = scatter_y(in_w)
    in_w, up_grad, down_got = after(in_w, up_grad, down_got)
    down_grad = dp_move(both_sum(down_own, down_got))
    tail = tail + swap(tail, "tp", 4, 1)
    tail = tail + swap(tail, "tp", 4, 2)
    tail_own, tail_got = scatter_y(tail)
    tail_size = tail.shape[1]
    tail_rows = -(-tail_size // (16 * w1)) * 16
    tail = jnp.pad(tail_own + tail_got, ((0, 0), (0, tail_rows * w1 - tail_size)))
    out_w = scatter_z(out_w)
    in_w = both_sum(*in_w)
    in_rows = in_w.shape[1]
    in_w = jnp.concatenate([in_w, tail.reshape(dp, tail_rows, w1).astype(BF16)], axis=1)
    in_w = jnp.sum(dp_move(in_w).astype(F32), axis=0)
    tail = in_w[in_rows:].reshape(-1)[:tail_size]
    in_w = in_w[:in_rows]
    g_po, g_ao = out_w[:, :d_slice], out_w[:, d_slice:]
    g_pq, g_aq = in_w[:d_slice, :q_cols], in_w[d_slice:, :q_cols]
    kv_w = in_w[:, q_cols:].astype(BF16)
    kv_other = swap(kv_w, "tp", 4, 1).astype(F32)
    kv_w = kv_w.astype(F32)
    kv_w = jnp.concatenate(
        [jnp.where(core == 0, kv_w, kv_other), jnp.where(core == 0, kv_other, kv_w)], axis=1
    )
    g_pkv, g_akv = kv_w[:d_slice], kv_w[d_slice:]

    out_pre, out_suf = undo_block(sum(outs))
    out_block = pack.join(resid + out_pre, resid_suf + out_suf).astype(BF16)
    out_pre, out_suf = pack.tp_gather(out_block)
    prefix_out = out_pre.reshape(pre_items, half_rows, width)
    suffix_out = out_suf[None, :suf_len]
    grad_pre, grad_suf = pack.tp_gather(pack.join(grad_mine, grad_suf_mine).astype(BF16))
    prefix_grad = grad_pre.astype(F32).reshape(pre_items, half_rows, width)
    suffix_grad = grad_suf.astype(F32)[None, :suf_len]
    g_pg, g_ag = columns_end(gate_grad)
    g_pu, g_au = columns_end(up_grad)
    g_pd = down_grad[:, :hid].reshape(dp * hid, d_slice).astype(F32)
    g_ad = halves_down(down_grad[:, hid:], 2).reshape(dp * hid_act, a_slice).astype(F32)
    tails, at = [], 0
    for size in (d_slice, d_slice, a_slice, a_slice, action_embed.size):
        tails.append(tail[at : at + size])
        at += size
    g_gpa, g_gpf, g_gaa, g_gaf, g_embed = tails
    g_embed = g_embed.reshape(action_embed.shape)
    return (
        prefix_out,
        suffix_out,
        prefix_grad,
        suffix_grad,
        g_pq,
        g_pkv,
        g_po,
        g_pg,
        g_pu,
        g_pd,
        g_gpa,
        g_gpf,
        g_aq,
        g_akv,
        g_ao,
        g_ag,
        g_au,
        g_ad,
        g_gaa,
        g_gaf,
        g_embed,
    )


def solution(mesh):
    return jax.shard_map(
        functools.partial(local, mesh.shape["dp"]),
        mesh=mesh,
        in_specs=(
            P("dp", "expert", None),
            P(("dp", "expert"), None, None),
            P(("dp", "expert"), None, None),
            P("dp"),
            P(("dp", "expert"), None),
            P(("dp", "expert"), "tp"),
            P(("dp", "expert"), None),
            P("tp", ("dp", "expert")),
            P(("dp", "expert"), "tp"),
            P(("dp", "expert"), "tp"),
            P("tp", ("dp", "expert")),
            P(("dp", "expert")),
            P(("dp", "expert")),
            P(("dp", "expert"), "tp"),
            P(("dp", "expert"), None),
            P("tp", ("dp", "expert")),
            P(("dp", "expert"), "tp"),
            P(("dp", "expert"), "tp"),
            P("tp", ("dp", "expert")),
            P(("dp", "expert")),
            P(("dp", "expert")),
            P(("dp", "expert"), None),
            P("dp", "expert", None),
            P(("dp", "expert"), None, None),
        ),
        out_specs=(
            P("dp", "expert", None),
            P(("dp", "expert"), None, None),
            P("dp", "expert", None),
            P(("dp", "expert"), None, None),
            P(("dp", "expert"), "tp"),
            P(("dp", "expert"), None),
            P("tp", ("dp", "expert")),
            P(("dp", "expert"), "tp"),
            P(("dp", "expert"), "tp"),
            P("tp", ("dp", "expert")),
            P(("dp", "expert")),
            P(("dp", "expert")),
            P(("dp", "expert"), "tp"),
            P(("dp", "expert"), None),
            P("tp", ("dp", "expert")),
            P(("dp", "expert"), "tp"),
            P(("dp", "expert"), "tp"),
            P("tp", ("dp", "expert")),
            P(("dp", "expert")),
            P(("dp", "expert")),
            P(("dp", "expert"), None),
        ),
        check_vma=False,
    )
```
